256 devices in a mesh: mem: 8 (over x, z_lo), tile: 32 (over z_hi, y, core).
Axes of the slice: x: 4, y: 4, z: 8 (z_hi: 4, z_lo: 2; z = z_hi * 2 + z_lo), core: 2. Of those that a mesh axis runs over, the one named last changes fastest.
Arguments:
- block_input: bfloat16 [16, 64, 256, 256], P('mem', None, 'tile'), may hold values from -36 to 36
- member_seeds: int32 [16], P('mem'), may hold values from 0 to 65520
- targets: float32 [2, 256, 256], P(None, 'tile'), may hold values from -6 to 6
- land_mask: int32 [256, 256], P('tile'), may hold values 0 or 1
- noise_weight: bfloat16 [64, 8], replicated, may hold values from -2 to 2
- conv_weight: bfloat16 [2, 9, 64, 64], replicated, may hold values from -0.25 to 0.25
- block_gain: float32 [2, 64], replicated, may hold values from 0.25 to 1.75
- head_weight: bfloat16 [2, 64], replicated, may hold values from -0.75 to 0.75
- head_gain: float32 [64], replicated, may hold values from 0.25 to 1.75
Outputs:
- energy_loss: float32 [], replicated
- predictions: float32 [16, 2, 256, 256], P('mem', None, 'tile')
- grad_conv: float32 [2, 9, 64, 64], replicated
- grad_block_gain: float32 [2, 64], replicated
- grad_head_weight: float32 [2, 64], replicated
- grad_head_gain: float32 [64], replicated
- grad_noise_weight: float32 [64, 8], replicated
The draws below stay inside these ranges and needn't reach their ends.
Inputs may be any that keep to these rules, and one draw needn't show every extreme that they name: `member_seeds`: each member's noise seed.
All inputs are finite; a program needn't handle non-finite values. No bound on the sum of `land_mask` on one device may be relied on, other than what follows from the above.
Results may differ from the reference program's by a relative error of at most 0.0034.
The reference program's roundings to bfloat16 on the way count: a program that leaves them out, or rounds other values in their place, can miss the bound.
Values may be sent and summed in bfloat16 or wider, within the bound.
A program may use at most 64 MiB of HBM per device.

```python
import math
import jax
import jax.numpy as jnp
from jax import lax

C = 64
NV = 2
NZ = 8
BLOCKS = 2
W = 256
LOSS_SCALE = 16384
MEMBERS = 16
H = 256


def draw_block_input(key, part):
    key = jax.random.fold_in(key, 11)
    key_chan, key_cell, key_main = jax.random.split(key, 3)
    channel_scale = jnp.exp(jax.random.uniform(key_chan, (MEMBERS, C, 1, 1), jnp.float32, math.log(0.3), math.log(3.0)))
    cell_scale = jnp.exp(jax.random.uniform(key_cell, (MEMBERS, 1, H, W), jnp.float32, math.log(0.3), math.log(3.0)))
    values = jax.random.truncated_normal(key_main, -4.0, 4.0, (MEMBERS, C, H, W), jnp.float32)
    return (values * channel_scale * cell_scale).astype(jnp.bfloat16)


def plant(values, rng, least, high):
    longest = values.shape.index(max(values.shape))
    spots = []
    for shift in (0, 1):
        where = [jax.random.randint(jax.random.fold_in(rng, axis), (), 0, length) for axis, length in enumerate(values.shape)]
        where[longest] = (where[longest] + shift) % values.shape[longest]
        spots.append(tuple(where))
    return values.at[spots[0]].set(least).at[spots[1]].set(high)


def shard_levels(rng, dims, cuts, smallest, largest):
    def one(axis_at, shards_of):
        heights = jax.random.uniform(jax.random.fold_in(jax.random.fold_in(rng, 6), axis_at), (shards_of,), jnp.float32, smallest / len(cuts), largest / len(cuts))
        return jnp.repeat(jnp.exp(heights), dims[axis_at] // shards_of).reshape((-1,) + (1,) * (len(dims) - axis_at - 1))

    loudness = one(*cuts[0])
    for cut in cuts[1:]:
        loudness = loudness * one(*cut)
    return loudness


def gaussian(rng, extent, scale, limit, shards=(), dtype=jnp.bfloat16):
    level = shard_levels(rng, extent, shards, -0.22, 0.18) if shards else 1.0
    entries = jax.random.normal(rng, extent, jnp.float32) * scale * level
    return jnp.minimum(jnp.maximum(entries, -limit), limit).astype(dtype)


def setup_inputs(seed: int = 0) -> dict:
    streams_of = jax.random.split(jax.random.key(seed), 10)
    block_input = draw_block_input(jax.random.fold_in(streams_of[9], 71), 0)
    member_seeds = plant(jax.random.randint(streams_of[1], (MEMBERS,), 0, 65521), jax.random.fold_in(streams_of[1], 1), 0, 65520).astype(jnp.int32)
    targets = gaussian(streams_of[2], (NV, H, W), 1.0, 6.0, ((1, 32),), jnp.float32)
    land_mask = plant((jax.random.randint(streams_of[3], (H, W), 0, 2) < 1).astype(jnp.int32), jax.random.fold_in(streams_of[3], 1), 0, 1)
    noise_weight = gaussian(streams_of[4], (C, NZ), NZ ** -0.5, 2.0)
    conv_weight = gaussian(streams_of[5], (BLOCKS, 9, C, C), (9 * C) ** -0.5, 0.25)
    block_gain = jnp.clip(1.0 + 0.15 * jax.random.normal(streams_of[6], (BLOCKS, C), jnp.float32), 0.25, 1.75)
    head_weight = gaussian(streams_of[7], (NV, C), C ** -0.5, 0.75)
    head_gain = jnp.clip(1.0 + 0.15 * jax.random.normal(streams_of[8], (C,), jnp.float32), 0.25, 1.75)
    return {"block_input": block_input, "member_seeds": member_seeds, "targets": targets, "land_mask": land_mask, "noise_weight": noise_weight, "conv_weight": conv_weight, "block_gain": block_gain, "head_weight": head_weight, "head_gain": head_gain}


eps_norm = 1e-05
smooth_sq = 0.01

def noise_field(seed_values, row_start, row_count, col_count, total_rows, channel_count):
    grid_shape = (seed_values.shape[0], channel_count, row_count, col_count)
    channel_ids = lax.broadcasted_iota(jnp.int32, grid_shape, 1)
    row_ids = jnp.clip(lax.broadcasted_iota(jnp.int32, grid_shape, 2) + row_start, 0, total_rows - 1)
    column_ids = lax.broadcasted_iota(jnp.int32, grid_shape, 3)
    section_one = (seed_values[:, None, None, None] + 7919 * channel_ids + row_ids * col_count + column_ids) % 65521
    section_two = (section_one * 3001 + 12345) % 65521
    folded = section_two % 46337
    section_three = (folded * folded + section_two) % 65521
    section_four = (section_three * 2897 + 4111) % 65521
    return ((section_four - 32760).astype(jnp.float32) / 18914.0).astype(jnp.bfloat16)

def ref_conv(padded, weights, row_count, col_count, transpose):
    channel_count = padded.shape[0]
    running = None
    for offset_r in range(3):
        for offset_c in range(3):
            if transpose:
                start_r = 2 - offset_r
                start_c = 2 - offset_c
                tap_weight = weights[3 * offset_r + offset_c].T
            else:
                start_r = offset_r
                start_c = offset_c
                tap_weight = weights[3 * offset_r + offset_c]
            window = padded[:, start_r:start_r + row_count, start_c:start_c + col_count].reshape(channel_count, -1)
            tap_term = jnp.dot(tap_weight, window, preferred_element_type=jnp.float32)
            running = tap_term if running is None else running + tap_term
    return running.reshape(-1, row_count, col_count)

def rms_parts(stream):
    rms_scale = jnp.sqrt(lax.optimization_barrier(jnp.mean(stream * stream, axis=0, keepdims=True)) + eps_norm)
    return (stream / rms_scale, rms_scale)

def norm_back(normed_grad, normed, rms_scale):
    return (normed_grad - normed * lax.optimization_barrier(jnp.mean(normed_grad * normed, axis=0, keepdims=True))) / rms_scale

def member_forward(input_one, seed_one, noise_weight, conv_weight, block_gain, head_weight, head_gain):
    noise_local = noise_field(seed_one[None], 0, H, W, H, NZ)[0]
    stream = input_one.astype(jnp.float32) + jnp.dot(noise_weight, noise_local.reshape(NZ, H * W), preferred_element_type=jnp.float32).reshape(C, H, W)
    stored = []
    for layer_index in range(BLOCKS):
        normed, rms_scale = rms_parts(stream)
        inputs = (normed * block_gain[layer_index][:, None, None]).astype(jnp.bfloat16)
        padded = jnp.pad(inputs, ((0, 0), (1, 1), (1, 1)))
        conv_out = ref_conv(padded, conv_weight[layer_index], H, W, False)
        stored.append((normed, rms_scale, padded, conv_out))
        stream = stream + jax.nn.silu(conv_out)
    normed, rms_scale = rms_parts(stream)
    head_in = (normed * head_gain[:, None, None]).astype(jnp.bfloat16)
    predictions = jnp.dot(head_weight, head_in.reshape(C, H * W), preferred_element_type=jnp.float32).reshape(NV, H, W)
    return (predictions, (noise_local, stored, normed, rms_scale, head_in))

def member_backward(input_one, seed_one, grad_one, noise_weight, conv_weight, block_gain, head_weight, head_gain):
    unused_pred, kept = member_forward(input_one, seed_one, noise_weight, conv_weight, block_gain, head_weight, head_gain)
    noise_local, stored, normed, rms_scale, head_in = kept
    flat_grad = grad_one.reshape(NV, H * W)
    grad_head_weight = jnp.dot(flat_grad, head_in.reshape(C, H * W).T, preferred_element_type=jnp.float32)
    head_in_grad = jnp.dot(head_weight.T, flat_grad, preferred_element_type=jnp.float32).reshape(C, H, W)
    grad_head_gain = lax.optimization_barrier(jnp.sum(head_in_grad * normed, axis=(1, 2)))
    stream_grad = norm_back(head_in_grad * head_gain[:, None, None], normed, rms_scale)
    conv_grads = []
    gain_grads = []
    for layer_index in reversed(range(BLOCKS)):
        normed_b, scale_b, padded_b, conv_out = stored[layer_index]
        sigmoid_out = jax.nn.sigmoid(conv_out)
        silu_slope = sigmoid_out * (1.0 + conv_out * (1.0 - sigmoid_out))
        conv_grad = (stream_grad * silu_slope).astype(jnp.bfloat16)
        padded_grad = jnp.pad(conv_grad, ((0, 0), (1, 1), (1, 1)))
        input_grad = ref_conv(padded_grad, conv_weight[layer_index], H, W, True)
        flat_conv = conv_grad.reshape(C, H * W)
        tap_grads = []
        for offset_r in range(3):
            for offset_c in range(3):
                window = padded_b[:, offset_r:offset_r + H, offset_c:offset_c + W].reshape(C, H * W)
                tap_grads.append(jnp.dot(flat_conv, window.T, preferred_element_type=jnp.float32))
        conv_grads.append(jnp.stack(tap_grads))
        gain_grads.append(lax.optimization_barrier(jnp.sum(input_grad * normed_b, axis=(1, 2))))
        stream_grad = stream_grad + norm_back(input_grad * block_gain[layer_index][:, None, None], normed_b, scale_b)
    entry_grad = stream_grad.astype(jnp.bfloat16)
    grad_noise_weight = jnp.dot(entry_grad.reshape(C, H * W), noise_local.reshape(NZ, H * W).T, preferred_element_type=jnp.float32)
    return (jnp.stack(conv_grads[::-1]), jnp.stack(gain_grads[::-1]), grad_head_weight, grad_head_gain, grad_noise_weight)

def reference(block_input, member_seeds, targets, land_mask, noise_weight, conv_weight, block_gain, head_weight, head_gain):

    def forward_only(pair_in):
        return member_forward(pair_in[0], pair_in[1], noise_weight, conv_weight, block_gain, head_weight, head_gain)[0]
    predictions = lax.map(forward_only, (block_input, member_seeds))
    row_float = lax.iota(jnp.int32, H).astype(jnp.float32)
    area_weight = 1.0 - 2.0 * row_float / (3.0 * H)
    weight = area_weight[:, None] * (1.0 + land_mask.astype(jnp.float32))
    misfit_diff = predictions - targets[None]
    misfit = jnp.sqrt(lax.optimization_barrier(jnp.sum(misfit_diff * misfit_diff, axis=1)) + smooth_sq)
    spread_const = jnp.sqrt(jnp.float32(smooth_sq))

    def pair_row(current):
        pred_diff = current[None] - predictions
        spread = jnp.sqrt(lax.optimization_barrier(jnp.sum(pred_diff * pred_diff, axis=1)) + smooth_sq)
        return (lax.optimization_barrier(jnp.sum(spread, axis=0)) - spread_const, lax.optimization_barrier(jnp.sum(pred_diff / spread[:, None], axis=0)))
    pair_total, pull_sum = lax.map(pair_row, predictions)
    pairs_norm = 2.0 * MEMBERS * (MEMBERS - 1)
    misfit_part = jnp.sum(weight[None] * misfit)
    pair_part = jnp.sum(weight[None] * pair_total)
    energy_loss = (misfit_part / MEMBERS - pair_part / pairs_norm) / (H * W)
    grad_coef = weight * (LOSS_SCALE / (H * W))
    pred_grad = (grad_coef[None, None] * (misfit_diff / misfit[:, None] / MEMBERS - pull_sum / (MEMBERS * (MEMBERS - 1.0)))).astype(jnp.bfloat16)

    def backward_one(triple_in):
        return member_backward(triple_in[0], triple_in[1], triple_in[2], noise_weight, conv_weight, block_gain, head_weight, head_gain)
    grads = lax.map(backward_one, (block_input, member_seeds, pred_grad))
    summed = jax.tree.map(lambda stacked: lax.optimization_barrier(jnp.sum(stacked, axis=0)), grads)
    return (energy_loss, predictions, summed[0], summed[1], summed[2], summed[3], summed[4])
```

```python
import jax
import jax.numpy as jnp
from jax import lax
from jax.experimental import pallas as pl
from jax.experimental.pallas import tpu as pltpu
from jax.sharding import PartitionSpec as P

LOSS_SCALE = 16384


MESH_ID = pl.DeviceIdType.MESH
GROUP = 16
eps_norm = 1e-05
smooth_sq = 0.01


def extended(cells, sides, width):
    for axis, dim in sides:
        count = lax.axis_size(axis)
        ends = count - 1
        head = lax.slice_in_dim(cells, 0, width, axis=dim)
        tail = lax.slice_in_dim(cells, cells.shape[dim] - width, cells.shape[dim], axis=dim)
        cells = jnp.concatenate(
            [
                lax.ppermute(tail, axis, [(i, (i + 1) % count) for i in range(ends)]),
                cells,
                lax.ppermute(head, axis, [((i + 1) % count, i) for i in range(ends)]),
            ],
            axis=dim,
        )
    return cells


def coordinates():
    mem, tile = lax.axis_index("mem"), lax.axis_index("tile")
    return mem // 2, (tile // 2) % 4, (tile // 8) * 2 + mem % 2, tile % 2


def device_at(x, y, z, core):
    return (x * 2 + z % 2, (z // 2) * 8 + y * 2 + core)


def plane_rank():
    x, y, _, _ = coordinates()
    return x * 4 + y


def plane_device(rank):
    _, _, z, core = coordinates()
    return device_at(rank // 4, rank % 4, z, core)


def line_rank():
    _, _, z, core = coordinates()
    return z * 2 + core


def line_device(rank):
    x, y, _, _ = coordinates()
    return device_at(x, y, rank // 2, rank % 2)


def others(rank):
    return [lax.rem(rank + step, GROUP) for step in range(1, GROUP)]


def sum_kernel(parts, out, mine, scattered, spread, plane_sems, line_sems, back_sems):
    in_plane, in_line = plane_rank(), line_rank()
    barrier = pltpu.get_barrier_semaphore()
    for rank in others(in_plane):
        pl.semaphore_signal(barrier, inc=1, device_id=plane_device(rank), device_id_type=MESH_ID)
    for rank in others(in_line):
        pl.semaphore_signal(barrier, inc=1, device_id=line_device(rank), device_id_type=MESH_ID)
    pl.semaphore_wait(barrier, 2 * (GROUP - 1))

    def exchange(ranks, device, source, target, sems):
        copies = []
        for step, rank in enumerate(ranks):
            copy = pltpu.make_async_remote_copy(
                src_ref=source(rank),
                dst_ref=target(step),
                send_sem=sems.at[0, step],
                recv_sem=sems.at[1, step],
                device_id=device(rank),
                device_id_type=MESH_ID,
            )
            copy.start()
            copies.append(copy)
        for copy in copies:
            copy.wait()

    exchange(
        others(in_plane),
        plane_device,
        lambda rank: parts.at[rank],
        lambda step: scattered.at[step],
        plane_sems,
    )
    total = parts[in_plane]
    for step in range(GROUP - 1):
        total = total + scattered[step]
    spread[in_line] = total
    exchange(
        others(in_line),
        line_device,
        lambda rank: spread.at[in_line],
        lambda step: spread.at[in_line],
        line_sems,
    )
    total = spread[0]
    for rank in range(1, GROUP):
        total = total + spread[rank]
    out[in_plane] = total
    exchange(
        others(in_plane),
        plane_device,
        lambda rank: out.at[in_plane],
        lambda step: out.at[in_plane],
        back_sems,
    )


def sum_everywhere(parts):
    rows = parts.shape[1]
    return pl.pallas_call(
        sum_kernel,
        out_shape=jax.ShapeDtypeStruct(parts.shape, jnp.float32),
        in_specs=[pl.BlockSpec(memory_space=pltpu.VMEM)],
        out_specs=pl.BlockSpec(memory_space=pltpu.VMEM),
        scratch_shapes=[
            pltpu.VMEM((rows, 128), jnp.float32),
            pltpu.VMEM((GROUP - 1, rows, 128), jnp.float32),
            pltpu.VMEM((GROUP, rows, 128), jnp.float32),
            pltpu.SemaphoreType.DMA((2, GROUP - 1)),
            pltpu.SemaphoreType.DMA((2, GROUP - 1)),
            pltpu.SemaphoreType.DMA((2, GROUP - 1)),
        ],
        compiler_params=pltpu.CompilerParams(
            collective_id=0, has_side_effects=True, vmem_limit_bytes=32 * 2**20
        ),
        name="sum_everywhere",
    )(parts)


def gather_kernel(own, out, send_sems, recv_sems):
    mem = lax.axis_index("mem")
    tile = lax.axis_index("tile")
    barrier = pltpu.get_barrier_semaphore()
    ranks = [lax.rem(mem + step, 8) for step in range(1, 8)]
    for rank in ranks:
        pl.semaphore_signal(barrier, inc=1, device_id=(rank, tile), device_id_type=MESH_ID)
    pl.semaphore_wait(barrier, 7)
    out[mem] = own[...]
    copies = []
    for step, rank in enumerate(ranks):
        copy = pltpu.make_async_remote_copy(
            src_ref=own,
            dst_ref=out.at[mem],
            send_sem=send_sems.at[step],
            recv_sem=recv_sems.at[step],
            device_id=(rank, tile),
            device_id_type=MESH_ID,
        )
        copy.start()
        copies.append(copy)
    for copy in copies:
        copy.wait()


def gather_members(own):
    return pl.pallas_call(
        gather_kernel,
        out_shape=jax.ShapeDtypeStruct((8,) + own.shape, jnp.float32),
        in_specs=[pl.BlockSpec(memory_space=pltpu.VMEM)],
        out_specs=pl.BlockSpec(memory_space=pltpu.VMEM),
        scratch_shapes=[pltpu.SemaphoreType.DMA((7,)), pltpu.SemaphoreType.DMA((7,))],
        compiler_params=pltpu.CompilerParams(
            collective_id=1, has_side_effects=True, vmem_limit_bytes=32 * 2**20
        ),
        name="gather_members",
    )(own)


def noise_field(seed_values, row_start, row_count, col_count, total_rows, channel_count):
    grid_shape = (seed_values.shape[0], channel_count, row_count, col_count)
    channel_ids = lax.broadcasted_iota(jnp.int32, grid_shape, 1)
    row_ids = jnp.clip(
        lax.broadcasted_iota(jnp.int32, grid_shape, 2) + row_start, 0, total_rows - 1
    )
    column_ids = lax.broadcasted_iota(jnp.int32, grid_shape, 3)
    section_one = (
        seed_values[:, None, None, None] + 7919 * channel_ids + row_ids * col_count + column_ids
    ) % 65521
    section_two = (section_one * 3001 + 12345) % 65521
    folded = section_two % 46337
    section_three = (folded * folded + section_two) % 65521
    section_four = (section_three * 2897 + 4111) % 65521
    return ((section_four - 32760).astype(jnp.float32) / 18914.0).astype(jnp.bfloat16)


def rms_parts(stream):
    rms_scale = jnp.sqrt(jnp.mean(stream * stream, axis=1, keepdims=True) + eps_norm)
    return (stream / rms_scale, rms_scale)


def norm_back(normed_grad, normed, rms_scale):
    return (
        normed_grad - normed * jnp.mean(normed_grad * normed, axis=1, keepdims=True)
    ) / rms_scale


def pad_columns(bordered):
    return jnp.pad(bordered, ((0, 0), (0, 0), (0, 0), (1, 1)))


def conv_rows(padded, weights, transpose):
    row_count = padded.shape[2] - 2
    col_count = padded.shape[3] - 2
    running = None
    for offset_r in range(3):
        for offset_c in range(3):
            if transpose:
                window = padded[
                    :,
                    :,
                    2 - offset_r : 2 - offset_r + row_count,
                    2 - offset_c : 2 - offset_c + col_count,
                ]
                tap_term = jnp.einsum(
                    "oi,morw->mirw",
                    weights[3 * offset_r + offset_c],
                    window,
                    preferred_element_type=jnp.float32,
                )
            else:
                window = padded[
                    :, :, offset_r : offset_r + row_count, offset_c : offset_c + col_count
                ]
                tap_term = jnp.einsum(
                    "oi,mirw->morw",
                    weights[3 * offset_r + offset_c],
                    window,
                    preferred_element_type=jnp.float32,
                )
            running = tap_term if running is None else running + tap_term
    return running


def on_device(
    block_input,
    member_seeds,
    targets,
    land_mask,
    noise_weight,
    conv_weight,
    block_gain,
    head_weight,
    head_gain,
):
    members_here, channels, row_count, col_count = block_input.shape
    blocks = conv_weight.shape[0]
    noise_count = noise_weight.shape[1]
    total_rows = row_count * lax.axis_size("tile")
    members_all = members_here * lax.axis_size("mem")
    row_start = lax.axis_index("tile") * row_count
    stored = []
    noise_local = noise_field(
        member_seeds, row_start, row_count, col_count, total_rows, noise_count
    )
    stream = block_input.astype(jnp.float32) + jnp.einsum(
        "ck,mkrw->mcrw", noise_weight, noise_local, preferred_element_type=jnp.float32
    )
    for layer_index in range(blocks):
        normed, rms_scale = rms_parts(stream)
        inputs = (normed * block_gain[layer_index][None, :, None, None]).astype(jnp.bfloat16)
        bordered = extended(inputs, (("tile", 2),), 1)
        padded = pad_columns(bordered)
        conv_out = conv_rows(padded, conv_weight[layer_index], False)
        stored.append((normed, rms_scale, padded, conv_out))
        stream = stream + jax.nn.silu(conv_out)
    normed, rms_scale = rms_parts(stream)
    head_in = (normed * head_gain[None, :, None, None]).astype(jnp.bfloat16)
    predictions = jnp.einsum(
        "vc,mcrw->mvrw", head_weight, head_in, preferred_element_type=jnp.float32
    )
    row_float = (lax.iota(jnp.int32, row_count) + row_start).astype(jnp.float32)
    area_weight = 1.0 - 2.0 * row_float / (3.0 * total_rows)
    weight = area_weight[:, None] * (1.0 + land_mask.astype(jnp.float32))
    misfit_diff = predictions - targets[None]
    misfit = jnp.sqrt(jnp.sum(misfit_diff * misfit_diff, axis=1) + smooth_sq)
    spread_const = jnp.sqrt(jnp.float32(smooth_sq))
    cells_all = total_rows * col_count
    pairs_norm = 2.0 * members_all * (members_all - 1)
    pred_diff = predictions[:, None] - gather_members(predictions).reshape((members_all,) + predictions.shape[1:])[None]
    spread = jnp.sqrt(jnp.sum(pred_diff * pred_diff, axis=2) + smooth_sq)
    pair_total = jnp.sum(spread, axis=1)
    pull_sum = jnp.sum(pred_diff / spread[:, :, None], axis=1)
    pair_part = jnp.sum(weight[None] * (pair_total - spread_const))
    misfit_part = jnp.sum(weight[None] * misfit)
    loss_part = (misfit_part / members_all - pair_part / pairs_norm) / cells_all
    grad_coef = weight * (LOSS_SCALE / cells_all)
    pred_grad = (
        grad_coef[None, None]
        * (
            misfit_diff / misfit[:, None] / members_all
            - pull_sum / (members_all * (members_all - 1.0))
        )
    ).astype(jnp.bfloat16)
    grad_head_weight = jnp.einsum(
        "mvrw,mcrw->vc", pred_grad, head_in, preferred_element_type=jnp.float32
    )
    head_in_grad = jnp.einsum(
        "vc,mvrw->mcrw", head_weight, pred_grad, preferred_element_type=jnp.float32
    )
    grad_head_gain = jnp.sum(head_in_grad * normed, axis=(0, 2, 3))
    stream_grad = norm_back(head_in_grad * head_gain[None, :, None, None], normed, rms_scale)
    conv_grads = []
    gain_grads = []
    for layer_index in reversed(range(blocks)):
        normed_b, scale_b, padded_b, conv_out = stored[layer_index]
        sigmoid_out = jax.nn.sigmoid(conv_out)
        silu_slope = sigmoid_out * (1.0 + conv_out * (1.0 - sigmoid_out))
        conv_grad = (stream_grad * silu_slope).astype(jnp.bfloat16)
        bordered_grad = extended(conv_grad, (("tile", 2),), 1)
        input_grad = conv_rows(pad_columns(bordered_grad), conv_weight[layer_index], True)
        tap_grads = []
        for offset_r in range(3):
            for offset_c in range(3):
                window = padded_b[
                    :, :, offset_r : offset_r + row_count, offset_c : offset_c + col_count
                ]
                tap_grads.append(
                    jnp.einsum(
                        "morw,mirw->oi", conv_grad, window, preferred_element_type=jnp.float32
                    )
                )
        conv_grads.append(jnp.stack(tap_grads))
        gain_grads.append(jnp.sum(input_grad * normed_b, axis=(0, 2, 3)))
        stream_grad = stream_grad + norm_back(
            input_grad * block_gain[layer_index][None, :, None, None], normed_b, scale_b
        )
    entry_grad = stream_grad.astype(jnp.bfloat16)
    grad_noise_weight = jnp.einsum(
        "mcrw,mkrw->ck", entry_grad, noise_local, preferred_element_type=jnp.float32
    )
    partials = (
        loss_part,
        jnp.stack(conv_grads[::-1]),
        jnp.stack(gain_grads[::-1]),
        grad_head_weight,
        grad_head_gain,
        grad_noise_weight,
    )
    flat = jnp.concatenate([part.reshape(-1) for part in partials])
    rows = -(-flat.size // (GROUP * 1024)) * 8
    packed = jnp.pad(flat, (0, GROUP * rows * 128 - flat.size)).reshape(GROUP, rows, 128)
    summed = sum_everywhere(packed).reshape(-1)
    totals, at = [], 0
    for part in partials:
        totals.append(summed[at : at + part.size].reshape(part.shape))
        at += part.size
    return (totals[0], predictions, totals[1], totals[2], totals[3], totals[4], totals[5])


def solution(mesh):
    return jax.shard_map(
        on_device,
        mesh=mesh,
        in_specs=(
            P("mem", None, "tile", None),
            P("mem"),
            P(None, "tile", None),
            P("tile", None),
            P(),
            P(),
            P(),
            P(),
            P(),
        ),
        out_specs=(P(), P("mem", None, "tile", None), P(), P(), P(), P(), P()),
        check_vma=False,
    )
```

```python
import jax
import jax.numpy as jnp
from jax import lax
from jax.experimental import pallas as pl
from jax.experimental.pallas import tpu as pltpu
from jax.sharding import PartitionSpec as P

LOSS_SCALE = 16384
MESH_ID = pl.DeviceIdType.MESH
GROUP = 16
MEMS = 8
TILES = 32
HERE = 2
MEMBERS = 16
ROWS = 8
COLS = 256
CH = 64
NOISE = 8
HALO = 4
EXT = ROWS + 2 * HALO
GRID_ROWS = ROWS * TILES
CHUNK = 24
F32 = jnp.float32
BF16 = jnp.bfloat16
eps_norm = 1e-05
smooth_sq = 0.01


def coordinates():
    mem, tile = lax.axis_index("mem"), lax.axis_index("tile")
    return mem // 2, (tile // 2) % 4, (tile // 8) * 2 + mem % 2, tile % 2


def device_at(x, y, z, core):
    return (x * 2 + z % 2, (z // 2) * 8 + y * 2 + core)


def plane_rank():
    x, y, _, _ = coordinates()
    return x * 4 + y


def plane_device(rank):
    _, _, z, core = coordinates()
    return device_at(rank // 4, rank % 4, z, core)


def line_rank():
    _, _, z, core = coordinates()
    return z * 2 + core


def line_device(rank):
    x, y, _, _ = coordinates()
    return device_at(x, y, rank // 2, rank % 2)


def mem_device(rank):
    return (rank, lax.axis_index("tile"))


def others(rank, count):
    return [lax.rem(rank + step, count) for step in range(1, count)]


def modulo(value, base):
    quotient = jnp.floor(value.astype(F32) * (1.0 / base)).astype(jnp.int32)
    rest = value - quotient * base
    rest = jnp.where(rest < 0, rest + base, rest)
    return jnp.where(rest >= base, rest - base, rest)


def noise_row(seed, row):
    channel = lax.broadcasted_iota(jnp.int32, (NOISE, COLS), 0)
    column = lax.broadcasted_iota(jnp.int32, (NOISE, COLS), 1)
    first = modulo(7919 * channel + column + (seed + row * COLS), 65521)
    second = modulo(first * 3001 + 12345, 65521)
    folded = modulo(second, 46337)
    third = modulo(folded * folded + second, 65521)
    fourth = modulo(third * 2897 + 4111, 65521)
    return ((fourth - 32760).astype(F32) / 18914.0).astype(BF16)


def columns_of(shape):
    return lax.broadcasted_iota(jnp.int32, shape, len(shape) - 1)


def from_left(value):
    return jnp.where(columns_of(value.shape) == 0, 0.0, pltpu.roll(value, 1, axis=1))


def from_right(value):
    return jnp.where(columns_of(value.shape) == COLS - 1, 0.0, pltpu.roll(value, COLS - 1, axis=1))


def dot(left, right):
    return jnp.dot(left, right, preferred_element_type=F32)


def dot_rows(left, right):
    return lax.dot_general(left, right, (((1,), (1,)), ((), ())), preferred_element_type=F32)


def diagonal():
    shape = (CH, CH)
    return lax.broadcasted_iota(jnp.int32, shape, 0) == lax.broadcasted_iota(jnp.int32, shape, 1)


def as_column(row):
    return jnp.sum(jnp.where(diagonal(), jnp.broadcast_to(row, (CH, CH)), 0.0), axis=1, keepdims=True)


def as_row(column):
    return jnp.sum(jnp.where(diagonal(), jnp.broadcast_to(column, (CH, CH)), 0.0), axis=0, keepdims=True)


def silu_parts(value):
    gate = 0.5 * jnp.tanh(0.5 * value) + 0.5
    gated = value * gate
    return gated, gate + gated * (1.0 - gate)


def inverse_scale(stream):
    return lax.rsqrt(jnp.sum(stream * stream, axis=0, keepdims=True) * (1.0 / CH) + eps_norm)


def norm_back(grad, normed, inverse):
    mean = jnp.sum(grad * normed, axis=0, keepdims=True) * (1.0 / CH)
    return (grad - normed * mean) * inverse


def step_kernel(
    block_input,
    seeds,
    targets,
    land_mask,
    noise_weight,
    conv_weight,
    block_gain,
    head_weight,
    head_gain,
    predictions,
    grad_conv,
    small_out,
    turned,
    raw,
    noise,
    stream0,
    stream1,
    stream2,
    inverse0,
    inverse1,
    inverse2,
    slope0,
    slope1,
    inputs0,
    inputs1,
    grads0,
    grads1,
    stream_grad,
    head_in,
    forward_taps,
    backward_taps,
    gains,
    edge_out,
    edge_in,
    target_tiles,
    weight_tiles,
    own_pred,
    all_pred,
    pred_grad,
    sums,
    tap_sum,
    parts,
    scattered,
    spread,
    gathered,
    whole,
    small,
    small_in,
    small_line,
    halo_sems,
    mem_sems,
    plane_sems,
    line_sems,
    back_sems,
    small_sems,
    small_line_sems,
):
    mem, tile = lax.axis_index("mem"), lax.axis_index("tile")
    in_plane, in_line = plane_rank(), line_rank()
    below, above = lax.rem(tile + 1, TILES), lax.rem(tile + TILES - 1, TILES)
    plane = [(plane_device(rank), rank) for rank in others(in_plane, GROUP)]
    line = [(line_device(rank), rank) for rank in others(in_line, GROUP)]
    members = [(mem_device(rank), rank) for rank in others(mem, MEMS)]

    barrier = pltpu.get_barrier_semaphore()
    for device in [(mem, below), (mem, above)] + [d for d, _ in plane + line + members]:
        pl.semaphore_signal(barrier, inc=1, device_id=device, device_id_type=MESH_ID)

    def send(source, target, sems, slot, device):
        copy = pltpu.make_async_remote_copy(
            src_ref=source,
            dst_ref=target,
            send_sem=sems.at[0, slot],
            recv_sem=sems.at[1, slot],
            device_id=device,
            device_id_type=MESH_ID,
        )
        copy.start()
        return copy

    def wait(copies):
        for copy in copies:
            copy.wait()

    for m in range(HERE):
        for half in range(2):
            lanes = pl.ds(128 * half, 128)
            turned[m, half] = block_input[m, :, :, lanes].astype(F32).reshape(CH * ROWS, 128)
            for r in range(ROWS):
                raw[HALO + r, m, :, lanes] = turned[m, half, pl.ds(r, CH, stride=ROWS), :].astype(BF16)
    for side, start in ((0, 0), (1, ROWS - 2)):
        edge_out[side] = jnp.zeros((8, COLS), F32)
        for v in range(2):
            edge_out[side, pl.ds(2 * v, 2), :] = targets[v, pl.ds(start, 2), :]
        edge_out[side, pl.ds(4, 2), :] = land_mask[pl.ds(start, 2), :].astype(F32)

    pl.semaphore_wait(barrier, 2 + 2 * (GROUP - 1) + (MEMS - 1))

    halo_copies = [
        send(raw.at[pl.ds(HALO, HALO)], raw.at[pl.ds(HALO + ROWS, HALO)], halo_sems, 0, (mem, above)),
        send(raw.at[pl.ds(ROWS, HALO)], raw.at[pl.ds(0, HALO)], halo_sems, 1, (mem, below)),
        send(edge_out.at[0], edge_in.at[1], halo_sems, 2, (mem, above)),
        send(edge_out.at[1], edge_in.at[0], halo_sems, 3, (mem, below)),
    ]

    unit = diagonal().astype(F32).astype(BF16)
    blank = jnp.zeros((CH, CH), BF16)
    for b in range(2):
        for dc in range(3):
            taps = [conv_weight[b, 3 * dr + dc] for dr in range(3)]
            turned_taps = [dot_rows(unit, tap).astype(BF16) for tap in taps]
            for ro in range(2):
                at = pl.ds((2 * dc + ro) * CH, CH)
                ahead = [blank] * ro + turned_taps + [blank] * (1 - ro)
                forward_taps[b, at, :] = dot_rows(unit, jnp.concatenate(ahead, axis=0)).astype(BF16)
                back = [blank] * ro + taps[::-1] + [blank] * (1 - ro)
                backward_taps[b, at, :] = dot_rows(unit, jnp.concatenate(back, axis=0)).astype(BF16)
    columns = [block_gain[pl.ds(0, 1), :], block_gain[pl.ds(1, 1), :], head_gain[...]]
    columns += [head_weight[pl.ds(v, 1), :].astype(F32) for v in range(2)]
    for at, row in enumerate(columns):
        gains[at] = jnp.broadcast_to(as_column(row), (CH, COLS))
    for at in range(5):
        sums[at] = jnp.zeros((CH, COLS), F32)
    sums_noise = [jnp.zeros((CH, NOISE), F32)]

    def inside(e):
        row = tile * ROWS - HALO + e
        return jnp.where((row >= 0) & (row < GRID_ROWS), 1.0, 0.0).astype(F32)

    def entry(e):
        row = jnp.clip(tile * ROWS - HALO + e, 0, GRID_ROWS - 1)
        for m in range(HERE):
            field = noise_row(seeds[m], row)
            noise[e, m] = field.astype(F32)
            stream = raw[e, m].astype(F32) + dot(noise_weight[...], field)
            stream0[e, m] = stream
            inverse = inverse_scale(stream)
            inverse0[e, m] = jnp.broadcast_to(inverse, (8, COLS))
            inputs0[e, m] = (stream * (inverse * inside(e)) * gains[0]).astype(BF16)

    def forward(b, e):
        source, stream_in, stream_out, slope = (
            (inputs0, stream0, stream1, slope0),
            (inputs1, stream1, stream2, slope1),
        )[b]
        for m in range(HERE):
            window = source[pl.ds(e - 1, 4), m].reshape(4 * CH, COLS)
            taken = dot(forward_taps[b], window)
            for ro in range(2):
                left, middle, right = [taken[(2 * dc + ro) * CH : (2 * dc + ro + 1) * CH] for dc in range(3)]
                gated, bent = silu_parts(middle + from_left(left) + from_right(right))
                slope[e + ro, m] = bent
                stream = stream_in[e + ro, m] + gated
                stream_out[e + ro, m] = stream
                inverse = inverse_scale(stream)
                if b == 0:
                    inverse1[e + ro, m] = jnp.broadcast_to(inverse, (8, COLS))
                    inputs1[e + ro, m] = (stream * (inverse * inside(e + ro)) * gains[1]).astype(BF16)
                else:
                    inverse2[e + ro, m] = jnp.broadcast_to(inverse, (8, COLS))
                    headed = (stream * inverse * gains[2]).astype(BF16)
                    head_in[e + ro, m] = headed
                    found = dot(head_weight[...], headed)
                    place(own_pred, m, e + ro, found)

    def spots(e):
        if isinstance(e, int) and not HALO <= e < HALO + ROWS:
            at = (e - 2) if e < HALO else (e - HALO - ROWS + 2)
            return [(2, at), (2, at + 4)]
        return [(0, e - HALO), (1, e - HALO)]

    def place(ref, m, e, pair):
        for v, (part, at) in enumerate(spots(e)):
            ref[m, part, pl.ds(at, 1), :] = pair[v : v + 1]

    def over(first, count, body):
        lax.fori_loop(0, count, lambda i, c: (body(first + 2 * i), c)[1], 0)

    def over_rows(first, count, body):
        lax.fori_loop(0, count, lambda i, c: (body(first + i), c)[1], 0)

    over_rows(HALO, ROWS, entry)
    over(5, 3, lambda e: forward(0, e))
    wait(halo_copies)
    over_rows(0, HALO, entry)
    over_rows(HALO + ROWS, HALO, entry)
    over(1, 2, lambda e: forward(0, e))
    over(11, 2, lambda e: forward(0, e))
    forward(1, 2)
    forward(1, 12)
    over(4, 4, lambda e: forward(1, e))

    all_pred[mem] = own_pred[...]
    pred_copies = [
        send(own_pred, all_pred.at[mem], mem_sems, step, device) for step, (device, _) in enumerate(members)
    ]
    predictions[...] = own_pred[:, pl.ds(0, 2)]
    for v in range(2):
        target_tiles[v] = targets[v]
        for side in range(2):
            target_tiles[2, pl.ds(4 * v + 2 * side, 2), :] = edge_in[side, pl.ds(2 * v, 2), :]
            weight_tiles[1, pl.ds(4 * v + 2 * side, 2), :] = edge_in[side, pl.ds(4, 2), :]
    weight_tiles[0] = land_mask[...].astype(F32)
    own_row = lax.broadcasted_iota(jnp.int32, (8, COLS), 0)
    side_row = own_row % 4
    side_row = jnp.where(side_row < 2, side_row - 2, side_row + ROWS - 2)
    for at, rows in enumerate((own_row, side_row)):
        area = 1.0 - 2.0 * (rows + tile * ROWS).astype(F32) / (3.0 * GRID_ROWS)
        weight_tiles[at] = area * (1.0 + weight_tiles[at])
    wait(pred_copies)

    def lengths(own, edge):
        squares = edge * edge
        return own[0] * own[0] + own[1] * own[1] + smooth_sq, squares + pltpu.roll(squares, 4, axis=0) + smooth_sq

    cells = GRID_ROWS * COLS
    loss_tile = jnp.zeros((8, COLS), F32)
    for m in range(HERE):
        mine = [own_pred[m, part] for part in range(3)]

        def pull_from(n, carry):
            pulls, total = carry
            gaps = [mine[part] - all_pred[n // HERE, lax.rem(n, HERE), part] for part in range(3)]
            own_sq, edge_sq = lengths(gaps[:2], gaps[2])
            own_inv, edge_inv = lax.rsqrt(own_sq), lax.rsqrt(edge_sq)
            pulls = tuple(
                pull + gap * inv for pull, gap, inv in zip(pulls, gaps, (own_inv, own_inv, edge_inv))
            )
            return pulls, total + own_sq * own_inv

        blank_tile = jnp.zeros((8, COLS), F32)
        pulls, total = lax.fori_loop(0, MEMBERS, pull_from, ((blank_tile,) * 3, blank_tile - smooth_sq**0.5))
        misses = [mine[part] - target_tiles[part] for part in range(3)]
        own_sq, edge_sq = lengths(misses[:2], misses[2])
        own_inv, edge_inv = lax.rsqrt(own_sq), lax.rsqrt(edge_sq)
        loss_tile += weight_tiles[0] * (
            own_sq * own_inv * (1.0 / MEMBERS) - total * (1.0 / (2.0 * MEMBERS * (MEMBERS - 1)))
        )
        for part, inv in enumerate((own_inv, own_inv, edge_inv)):
            factor = weight_tiles[part // 2] * (LOSS_SCALE / cells)
            grad = factor * (
                misses[part] * inv * (1.0 / MEMBERS) - pulls[part] * (1.0 / (MEMBERS * (MEMBERS - 1.0)))
            )
            pred_grad[m, part] = grad.astype(BF16).astype(F32)

    def top(e, own):
        for m in range(HERE):
            (part0, at0), (part1, at1) = spots(e)
            pull0 = pred_grad[m, part0, pl.ds(at0, 1), :]
            pull1 = pred_grad[m, part1, pl.ds(at1, 1), :]
            grad = gains[3] * pull0 + gains[4] * pull1
            inverse = inverse2[e, m, pl.ds(0, 1), :]
            normed = stream2[e, m] * inverse
            if own:
                headed = head_in[e, m].astype(F32)
                sums[2] += grad * normed
                sums[3] += headed * pull0
                sums[4] += headed * pull1
            grad = norm_back(grad * gains[2], normed, inverse)
            stream_grad[e, m] = grad
            grads1[e, m] = (grad * (slope1[e, m] * inside(e))).astype(BF16)

    def tap_grads(grads, inputs):
        tap_sum[...] = jnp.zeros_like(tap_sum)

        def one(e):
            for m in range(HERE):
                grad = grads[e, m].astype(F32)
                shifts = [from_right(grad), grad, from_left(grad)]
                shifts = jnp.concatenate([shift.astype(BF16) for shift in shifts], axis=0)
                window = inputs[pl.ds(e - 1, 3), m].reshape(3 * CH, COLS)
                tap_sum[:, pl.ds(0, 3 * CH)] += dot_rows(shifts, window)

        over_rows(HALO, ROWS, one)

    def backward(b, e, last):
        source, stream, inverses = ((grads0, stream0, inverse0), (grads1, stream1, inverse1))[b]
        for m in range(HERE):
            window = source[pl.ds(e - 1, 4), m].reshape(4 * CH, COLS)
            taken = dot(backward_taps[b], window)
            for ro in range(2):
                left, middle, right = [taken[(2 * dc + ro) * CH : (2 * dc + ro + 1) * CH] for dc in range(3)]
                grad = middle + from_right(left) + from_left(right)
                inverse = inverses[e + ro, m, pl.ds(0, 1), :]
                normed = stream[e + ro, m] * inverse
                counted = jnp.where((e + ro >= HALO) & (e + ro < HALO + ROWS), 1.0, 0.0).astype(F32)
                sums[b] += grad * (normed * counted)
                total = stream_grad[e + ro, m] + norm_back(grad * gains[b], normed, inverse)
                if b == 1:
                    stream_grad[e + ro, m] = total
                    grads0[e + ro, m] = (total * (slope0[e + ro, m] * inside(e + ro))).astype(BF16)
                else:
                    last(e + ro, m, total.astype(BF16))

    def to_parts(b):
        for at in range(GROUP):
            parts[b, at] = tap_sum[pl.ds(CHUNK * (at // 2), CHUNK), pl.ds(128 * (at % 2), 128)]

    def scatter(b):
        return [
            send(parts.at[b, rank], scattered.at[b, step], plane_sems.at[b], step, device)
            for step, (device, rank) in enumerate(plane)
        ]

    def spread_out(b):
        total = parts[b, in_plane]
        for step in range(GROUP - 1):
            total = total + scattered[b, step]
        spread[b, in_line] = total
        return [
            send(spread.at[b, in_line], spread.at[b, in_line], line_sems.at[b], step, device)
            for step, (device, _) in enumerate(line)
        ]

    def gather(b):
        total = spread[b, 0]
        for rank in range(1, GROUP):
            total = total + spread[b, rank]
        gathered[b, in_plane] = total
        return [
            send(gathered.at[b, in_plane], gathered.at[b, in_plane], back_sems.at[b], step, device)
            for step, (device, _) in enumerate(plane)
        ]

    def finish(b):
        for at in range(GROUP):
            whole[pl.ds(CHUNK * (at // 2), CHUNK), pl.ds(128 * (at % 2), 128)] = gathered[b, at]
        for dr in range(3):
            for dc in range(3):
                grad_conv[b, 3 * dr + dc] = whole[pl.ds(CH * dc, CH), pl.ds(CH * dr, CH)]

    for e in (2, 3, 12, 13):
        top(e, False)
    over_rows(HALO, ROWS, lambda e: top(e, True))
    tap_grads(grads1, inputs1)
    to_parts(1)
    plane_1 = scatter(1)
    over(3, 5, lambda e: backward(1, e, None))
    tap_grads(grads0, inputs0)
    to_parts(0)
    plane_0 = scatter(0)
    wait(plane_1)
    line_1 = spread_out(1)

    small[...] = jnp.zeros_like(small)
    sum_noise = tap_sum.at[pl.ds(0, CH), pl.ds(0, NOISE)]
    sum_noise[...] = jnp.zeros((CH, NOISE), F32)

    def last(e, m, entry_grad):
        sum_noise[...] += dot_rows(entry_grad, noise[e, m].astype(BF16))

    over(4, 4, lambda e: backward(0, e, last))
    column = lax.broadcasted_iota(jnp.int32, (CH, NOISE), 1)
    late = sum_noise[...]
    for at in range(5):
        small[pl.ds(at, 1), pl.ds(0, CH)] = as_row(jnp.sum(sums[at], axis=1, keepdims=True))
    for k in range(NOISE):
        picked = jnp.sum(jnp.where(column == k, late, 0.0), axis=1, keepdims=True)
        small[pl.ds(5 + k, 1), pl.ds(0, CH)] = as_row(picked)
    loss = jnp.sum(jnp.sum(loss_tile, axis=0, keepdims=True), axis=1, keepdims=True) * (1.0 / cells)
    small[pl.ds(13, 1), :] = jnp.broadcast_to(loss, (1, 128))
    small_in[in_plane] = small[...]
    small_1 = [
        send(small, small_in.at[in_plane], small_sems, step, device) for step, (device, _) in enumerate(plane)
    ]
    wait(plane_0)
    line_0 = spread_out(0)
    wait(line_1)
    back_1 = gather(1)
    wait(small_1)
    total = small_in[0]
    for rank in range(1, GROUP):
        total = total + small_in[rank]
    small_line[in_line] = total
    small_2 = [
        send(small_line.at[in_line], small_line.at[in_line], small_line_sems, step, device)
        for step, (device, _) in enumerate(line)
    ]
    wait(line_0)
    back_0 = gather(0)
    wait(back_1)
    finish(1)
    wait(small_2)
    total = small_line[0]
    for rank in range(1, GROUP):
        total = total + small_line[rank]
    small_out[...] = total
    wait(back_0)
    finish(0)


def on_device(
    block_input,
    member_seeds,
    targets,
    land_mask,
    noise_weight,
    conv_weight,
    block_gain,
    head_weight,
    head_gain,
):
    vmem = pl.BlockSpec(memory_space=pltpu.VMEM)
    smem = pl.BlockSpec(memory_space=pltpu.SMEM)

    def field(*shape):
        return pltpu.VMEM((EXT, HERE) + shape, F32)

    def half(*shape):
        return pltpu.VMEM((EXT, HERE) + shape, BF16)

    def sems(*shape):
        return pltpu.SemaphoreType.DMA(shape)

    scratch = dict(
        turned=pltpu.VMEM((HERE, 2, CH * ROWS, 128), F32),
        raw=half(CH, COLS),
        noise=field(NOISE, COLS),
        stream0=field(CH, COLS),
        stream1=field(CH, COLS),
        stream2=field(CH, COLS),
        inverse0=field(8, COLS),
        inverse1=field(8, COLS),
        inverse2=field(8, COLS),
        slope0=field(CH, COLS),
        slope1=field(CH, COLS),
        inputs0=half(CH, COLS),
        inputs1=half(CH, COLS),
        grads0=half(CH, COLS),
        grads1=half(CH, COLS),
        stream_grad=field(CH, COLS),
        head_in=half(CH, COLS),
        forward_taps=pltpu.VMEM((2, 6 * CH, 4 * CH), BF16),
        backward_taps=pltpu.VMEM((2, 6 * CH, 4 * CH), BF16),
        gains=pltpu.VMEM((5, CH, COLS), F32),
        edge_out=pltpu.VMEM((2, 8, COLS), F32),
        edge_in=pltpu.VMEM((2, 8, COLS), F32),
        target_tiles=pltpu.VMEM((3, 8, COLS), F32),
        weight_tiles=pltpu.VMEM((2, 8, COLS), F32),
        own_pred=pltpu.VMEM((HERE, 3, 8, COLS), F32),
        all_pred=pltpu.VMEM((MEMS, HERE, 3, 8, COLS), F32),
        pred_grad=pltpu.VMEM((HERE, 3, 8, COLS), F32),
        sums=pltpu.VMEM((5, CH, COLS), F32),
        tap_sum=pltpu.VMEM((3 * CH, 256), F32),
        parts=pltpu.VMEM((2, GROUP, CHUNK, 128), F32),
        scattered=pltpu.VMEM((2, GROUP - 1, CHUNK, 128), F32),
        spread=pltpu.VMEM((2, GROUP, CHUNK, 128), F32),
        gathered=pltpu.VMEM((2, GROUP, CHUNK, 128), F32),
        whole=pltpu.VMEM((3 * CH, 256), F32),
        small=pltpu.VMEM((16, 128), F32),
        small_in=pltpu.VMEM((GROUP, 16, 128), F32),
        small_line=pltpu.VMEM((GROUP, 16, 128), F32),
        halo_sems=sems(2, 4),
        mem_sems=sems(2, MEMS - 1),
        plane_sems=sems(2, 2, GROUP - 1),
        line_sems=sems(2, 2, GROUP - 1),
        back_sems=sems(2, 2, GROUP - 1),
        small_sems=sems(2, GROUP - 1),
        small_line_sems=sems(2, GROUP - 1),
    )
    predictions, grad_conv, small = pl.pallas_call(
        step_kernel,
        out_shape=(
            jax.ShapeDtypeStruct((HERE, 2, ROWS, COLS), F32),
            jax.ShapeDtypeStruct((2, 9, CH, CH), F32),
            jax.ShapeDtypeStruct((16, 128), F32),
        ),
        in_specs=[vmem, smem] + [vmem] * 7,
        out_specs=(vmem, vmem, vmem),
        scratch_shapes=list(scratch.values()),
        compiler_params=pltpu.CompilerParams(
            collective_id=0, has_side_effects=True, vmem_limit_bytes=48 * 2**20
        ),
        name="train_step",
    )(
        block_input,
        member_seeds,
        targets,
        land_mask,
        noise_weight,
        conv_weight,
        block_gain,
        head_weight,
        head_gain.reshape(1, CH),
    )
    return (
        small[13, 0],
        predictions,
        grad_conv,
        small[0:2, :CH],
        small[3:5, :CH],
        small[2, :CH],
        small[5:13, :CH].T,
    )


def solution(mesh):
    return jax.shard_map(
        on_device,
        mesh=mesh,
        in_specs=(
            P("mem", None, "tile", None),
            P("mem"),
            P(None, "tile", None),
            P("tile", None),
            P(),
            P(),
            P(),
            P(),
            P(),
        ),
        out_specs=(P(), P("mem", None, "tile", None), P(), P(), P(), P(), P()),
        check_vma=False,
    )
```

```python
import jax
import jax.numpy as jnp
from jax import lax
from jax.experimental import pallas as pl
from jax.experimental.pallas import tpu as pltpu
from jax.sharding import PartitionSpec as P

LOSS_SCALE = 16384
MESH_ID = pl.DeviceIdType.MESH
GROUP = 16
MEMS = 8
TILES = 32
HERE = 2
MEMBERS = 16
ROWS = 8
COLS = 256
CH = 64
NOISE = 8
HALO = 4
EXT = ROWS + 2 * HALO
GRID_ROWS = ROWS * TILES
CHUNK = 24
VMEM_BYTES = 63 * 2**20
F32 = jnp.float32
BF16 = jnp.bfloat16
eps_norm = 1e-05
smooth_sq = 0.01


def coordinates():
    mem, tile = lax.axis_index("mem"), lax.axis_index("tile")
    return mem // 2, (tile // 2) % 4, (tile // 8) * 2 + mem % 2, tile % 2


def device_at(x, y, z, core):
    return (x * 2 + z % 2, (z // 2) * 8 + y * 2 + core)


def plane_rank():
    x, y, _, _ = coordinates()
    return x * 4 + y


def plane_device(rank):
    _, _, z, core = coordinates()
    return device_at(rank // 4, rank % 4, z, core)


def line_rank():
    _, _, z, core = coordinates()
    return z * 2 + core


def line_device(rank):
    x, y, _, _ = coordinates()
    return device_at(x, y, rank // 2, rank % 2)


def mem_device(rank):
    return (rank, lax.axis_index("tile"))


def others(rank, count):
    return [lax.rem(rank + step, count) for step in range(1, count)]


def modulo(value, base):
    quotient = jnp.floor(value.astype(F32) * (1.0 / base)).astype(jnp.int32)
    rest = value - quotient * base
    rest = jnp.where(rest < 0, rest + base, rest)
    return jnp.where(rest >= base, rest - base, rest)


def noise_row(seed, row):
    channel = lax.broadcasted_iota(jnp.int32, (NOISE, COLS), 0)
    column = lax.broadcasted_iota(jnp.int32, (NOISE, COLS), 1)
    first = modulo(7919 * channel + column + (seed + row * COLS), 65521)
    second = modulo(first * 3001 + 12345, 65521)
    folded = modulo(second, 46337)
    third = modulo(folded * folded + second, 65521)
    fourth = modulo(third * 2897 + 4111, 65521)
    return ((fourth - 32760).astype(F32) / 18914.0).astype(BF16)


def columns_of(shape):
    return lax.broadcasted_iota(jnp.int32, shape, len(shape) - 1)


def from_left(value):
    return jnp.where(columns_of(value.shape) == 0, jnp.zeros((), value.dtype), pltpu.roll(value, 1, axis=1))


def from_right(value):
    return jnp.where(
        columns_of(value.shape) == COLS - 1, jnp.zeros((), value.dtype), pltpu.roll(value, COLS - 1, axis=1)
    )


def dot(left, right):
    return jnp.dot(left, right, preferred_element_type=F32)


def dot_rows(left, right):
    return lax.dot_general(left, right, (((1,), (1,)), ((), ())), preferred_element_type=F32)


def diagonal():
    shape = (CH, CH)
    return lax.broadcasted_iota(jnp.int32, shape, 0) == lax.broadcasted_iota(jnp.int32, shape, 1)


def as_column(row):
    return jnp.sum(jnp.where(diagonal(), jnp.broadcast_to(row, (CH, CH)), 0.0), axis=1, keepdims=True)


def as_row(column):
    return jnp.sum(jnp.where(diagonal(), jnp.broadcast_to(column, (CH, CH)), 0.0), axis=0, keepdims=True)


def silu_parts(value):
    gate = 0.5 * jnp.tanh(0.5 * value) + 0.5
    gated = value * gate
    return gated, gate + gated * (1.0 - gate)


def inverse_scale(stream):
    return lax.rsqrt(jnp.sum(stream * stream, axis=0, keepdims=True) * (1.0 / CH) + eps_norm)


def norm_back(grad, normed, inverse):
    mean = jnp.sum(grad * normed, axis=0, keepdims=True) * (1.0 / CH)
    return (grad - normed * mean) * inverse


def step_kernel(
    block_input_far,
    seeds_far,
    targets_far,
    land_mask_far,
    noise_weight_far,
    conv_weight_far,
    block_gain_far,
    head_weight_far,
    head_gain_far,
    predictions,
    gathered,
    small_out,
    block_input,
    seeds,
    targets,
    land_mask,
    noise_weight,
    conv_weight,
    block_gain,
    head_weight,
    head_gain,
    load_sems,
    turned,
    raw,
    noise,
    stream0,
    stream1,
    stream2,
    inverse0,
    inverse1,
    inverse2,
    slope0,
    slope1,
    inputs0,
    inputs1,
    grads0,
    grads1,
    stream_grad,
    head_in,
    forward_taps,
    backward_taps,
    noise_taps,
    gains,
    edge_out,
    edge_in,
    target_tiles,
    weight_tiles,
    own_pred,
    all_pred,
    pred_grad,
    sums,
    tap_sum,
    parts,
    scattered,
    spread,
    small,
    small_in,
    small_line,
    halo_sems,
    mem_sems,
    plane_sems,
    line_sems,
    back_sems,
    small_sems,
    small_line_sems,
):
    mem, tile = lax.axis_index("mem"), lax.axis_index("tile")
    in_plane, in_line = plane_rank(), line_rank()
    below, above = lax.rem(tile + 1, TILES), lax.rem(tile + TILES - 1, TILES)
    plane = [(plane_device(rank), rank) for rank in others(in_plane, GROUP)]
    line = [(line_device(rank), rank) for rank in others(in_line, GROUP)]
    groups, ranks = ((plane, line), (line, plane)), ((in_plane, in_line), (in_line, in_plane))
    members = [(mem_device(rank), rank) for rank in others(mem, MEMS)]

    loads = [
        pltpu.make_async_copy(far, near, load_sems.at[at])
        for at, (far, near) in enumerate(
            (
                (block_input_far, block_input),
                (seeds_far, seeds),
                (targets_far, targets),
                (land_mask_far, land_mask),
                (noise_weight_far, noise_weight),
                (conv_weight_far, conv_weight),
                (block_gain_far, block_gain),
                (head_weight_far, head_weight),
                (head_gain_far, head_gain),
            )
        )
    ]
    for load in loads:
        load.start()

    barrier = pltpu.get_barrier_semaphore()
    for device in [(mem, below), (mem, above)] + [d for d, _ in plane + line + members]:
        pl.semaphore_signal(barrier, inc=1, device_id=device, device_id_type=MESH_ID)

    def send(source, target, sems, slot, device):
        copy = pltpu.make_async_remote_copy(
            src_ref=source,
            dst_ref=target,
            send_sem=sems.at[0, slot],
            recv_sem=sems.at[1, slot],
            device_id=device,
            device_id_type=MESH_ID,
        )
        copy.start()
        return copy

    def wait(copies):
        for copy in copies:
            copy.wait()

    wait(loads)
    for m in range(HERE):
        for half in range(2):
            lanes = pl.ds(128 * half, 128)
            turned[m, half] = block_input[m, :, :, lanes].astype(F32).reshape(CH * ROWS, 128)
            for r in range(ROWS):
                raw[HALO + r, m, :, lanes] = turned[m, half, pl.ds(r, CH, stride=ROWS), :].astype(BF16)
    for side, start in ((0, 0), (1, ROWS - 2)):
        edge_out[side] = jnp.zeros((8, COLS), F32)
        for v in range(2):
            edge_out[side, pl.ds(2 * v, 2), :] = targets[v, pl.ds(start, 2), :]
        edge_out[side, pl.ds(4, 2), :] = land_mask[pl.ds(start, 2), :].astype(F32)

    pl.semaphore_wait(barrier, 2 + 2 * (GROUP - 1) + (MEMS - 1))

    def halo(up, down, up_to, down_to, slot):
        return [
            send(raw.at[pl.ds(up, 2)], raw.at[pl.ds(up_to, 2)], halo_sems, slot, (mem, above)),
            send(raw.at[pl.ds(down, 2)], raw.at[pl.ds(down_to, 2)], halo_sems, slot + 1, (mem, below)),
        ]

    near_copies = halo(4, 10, 12, 2, 0)
    near_copies += [
        send(edge_out.at[0], edge_in.at[1], halo_sems, 4, (mem, above)),
        send(edge_out.at[1], edge_in.at[0], halo_sems, 5, (mem, below)),
    ]
    far_copies = halo(6, 8, 14, 0, 2)

    unit = diagonal().astype(F32).astype(BF16)
    blank = jnp.zeros((CH, CH), BF16)
    for b in range(2):
        for dc in range(3):
            taps = [conv_weight[b, 3 * dr + dc] for dr in range(3)]
            turned_taps = [dot_rows(unit, tap).astype(BF16) for tap in taps]
            for ro in range(2):
                at = pl.ds((2 * dc + ro) * CH, CH)
                ahead = [blank] * ro + turned_taps + [blank] * (1 - ro)
                forward_taps[b, at, :] = dot_rows(unit, jnp.concatenate(ahead, axis=0)).astype(BF16)
                back = [blank] * ro + taps[::-1] + [blank] * (1 - ro)
                backward_taps[b, at, :] = dot_rows(unit, jnp.concatenate(back, axis=0)).astype(BF16)
    noise_taps[...] = dot_rows(unit, noise_weight[...]).astype(BF16)
    columns = [block_gain[pl.ds(0, 1), :], block_gain[pl.ds(1, 1), :], head_gain[...]]
    columns += [head_weight[pl.ds(v, 1), :].astype(F32) for v in range(2)]
    for at, row in enumerate(columns):
        gains[at] = jnp.broadcast_to(as_column(row), (CH, COLS))
    for at in range(5):
        sums[at] = jnp.zeros((CH, COLS), F32)
    tap_sum[...] = jnp.zeros_like(tap_sum)

    def inside(e):
        row = tile * ROWS - HALO + e
        return jnp.where((row >= 0) & (row < GRID_ROWS), 1.0, 0.0).astype(F32)

    def make_noise(e):
        row = jnp.clip(tile * ROWS - HALO + e, 0, GRID_ROWS - 1)
        for m in range(HERE):
            noise[e, m] = noise_row(seeds[m], row).astype(F32)

    def entry(e):
        for m in range(HERE):
            stream = raw[e, m].astype(F32) + dot(noise_taps[...], noise[e, m].astype(BF16))
            stream0[e, m] = stream
            inverse = inverse_scale(stream)
            inverse0[e, m] = jnp.broadcast_to(inverse, (8, COLS))
            inputs0[e, m] = (stream * (inverse * inside(e)) * gains[0]).astype(BF16)

    def forward(b, e, ms=range(HERE)):
        source, stream_in, stream_out, slope = (
            (inputs0, stream0, stream1, slope0),
            (inputs1, stream1, stream2, slope1),
        )[b]
        for m in ms:
            window = source[pl.ds(e - 1, 4), m].reshape(4 * CH, COLS)
            taken = dot(forward_taps[b], window)
            for ro in range(2):
                left, middle, right = [taken[(2 * dc + ro) * CH : (2 * dc + ro + 1) * CH] for dc in range(3)]
                gated, bent = silu_parts(middle + from_left(left) + from_right(right))
                slope[e + ro, m] = bent
                stream = stream_in[e + ro, m] + gated
                stream_out[e + ro, m] = stream
                inverse = inverse_scale(stream)
                if b == 0:
                    inverse1[e + ro, m] = jnp.broadcast_to(inverse, (8, COLS))
                    inputs1[e + ro, m] = (stream * (inverse * inside(e + ro)) * gains[1]).astype(BF16)
                else:
                    inverse2[e + ro, m] = jnp.broadcast_to(inverse, (8, COLS))
                    headed = (stream * inverse * gains[2]).astype(BF16)
                    head_in[e + ro, m] = headed
                    found = dot(head_weight[...], headed)
                    place(own_pred, m, e + ro, found)

    def spots(e):
        if isinstance(e, int) and not HALO <= e < HALO + ROWS:
            at = (e - 2) if e < HALO else (e - HALO - ROWS + 2)
            return [(2, at), (2, at + 4)]
        return [(0, e - HALO), (1, e - HALO)]

    def place(ref, m, e, pair):
        for v, (part, at) in enumerate(spots(e)):
            ref[part, m, pl.ds(at, 1), :] = pair[v : v + 1]

    def over(first, count, body):
        for i in range(count):
            body(first + 2 * i)

    def over_rows(first, count, body):
        for i in range(count):
            body(first + i)

    def share(first, count, sems):
        parts_here = pl.ds(first, count)
        all_pred[mem, parts_here] = own_pred[parts_here]
        return [
            send(own_pred.at[parts_here], all_pred.at[mem, parts_here], sems, step, device)
            for step, (device, _) in enumerate(members)
        ]

    over_rows(HALO, ROWS, make_noise)
    over_rows(HALO, ROWS, entry)
    over(5, 3, lambda e: forward(0, e))
    over(6, 2, lambda e: forward(1, e))
    over_rows(0, HALO, make_noise)
    over_rows(HALO + ROWS, HALO, make_noise)
    wait(near_copies)
    for e in (2, 3, 12, 13):
        entry(e)
    for b, e in ((0, 3), (0, 11), (1, 4), (1, 10)):
        forward(b, e)
    own_copies = share(0, 2, mem_sems.at[0])
    for v in range(2):
        for m in range(HERE):
            predictions[m, v] = own_pred[v, m]
        target_tiles[v] = targets[v]
        for side in range(2):
            target_tiles[2, pl.ds(4 * v + 2 * side, 2), :] = edge_in[side, pl.ds(2 * v, 2), :]
            weight_tiles[1, pl.ds(4 * v + 2 * side, 2), :] = edge_in[side, pl.ds(4, 2), :]
    weight_tiles[0] = land_mask[...].astype(F32)
    wait(far_copies)
    for e in (0, 1, 14, 15):
        entry(e)
    for b, e in ((0, 1), (0, 13), (1, 2), (1, 12)):
        forward(b, e)
    edge_copies = share(2, 1, mem_sems.at[1])

    own_row = lax.broadcasted_iota(jnp.int32, (8, COLS), 0)
    side_row = own_row % 4
    side_row = jnp.where(side_row < 2, side_row - 2, side_row + ROWS - 2)
    for at, rows in enumerate((own_row, side_row)):
        area = 1.0 - 2.0 * (rows + tile * ROWS).astype(F32) / (3.0 * GRID_ROWS)
        weight_tiles[at] = area * (1.0 + weight_tiles[at])

    cells = GRID_ROWS * COLS

    def length_sq(gaps):
        if len(gaps) == 2:
            return gaps[0] * gaps[0] + gaps[1] * gaps[1] + smooth_sq
        squares = gaps[0] * gaps[0]
        return squares + pltpu.roll(squares, 4, axis=0) + smooth_sq

    def pull_apart(m, parts_here, weights):
        mine = [own_pred[part, m] for part in parts_here]
        pulls = [jnp.zeros((8, COLS), F32) for _ in parts_here]
        total = jnp.zeros((8, COLS), F32) - smooth_sq**0.5
        for n in range(MEMBERS):
            gaps = [own - all_pred[n // HERE, part, n % HERE] for own, part in zip(mine, parts_here)]
            square = length_sq(gaps)
            inverse = lax.rsqrt(square)
            pulls = [pull + gap * inverse for pull, gap in zip(pulls, gaps)]
            total = total + square * inverse
        misses = [own - target_tiles[part] for own, part in zip(mine, parts_here)]
        square = length_sq(misses)
        inverse = lax.rsqrt(square)
        factor = weights * (LOSS_SCALE / cells)
        for part, miss, pull in zip(parts_here, misses, pulls):
            grad = factor * (
                miss * inverse * (1.0 / MEMBERS) - pull * (1.0 / (MEMBERS * (MEMBERS - 1.0)))
            )
            pred_grad[part, m] = grad.astype(BF16).astype(F32)
        return weights * (
            square * inverse * (1.0 / MEMBERS) - total * (1.0 / (2.0 * MEMBERS * (MEMBERS - 1)))
        )

    def top(e, own):
        for m in range(HERE):
            (part0, at0), (part1, at1) = spots(e)
            pull0 = pred_grad[part0, m, pl.ds(at0, 1), :]
            pull1 = pred_grad[part1, m, pl.ds(at1, 1), :]
            grad = gains[3] * pull0 + gains[4] * pull1
            inverse = inverse2[e, m, pl.ds(0, 1), :]
            normed = stream2[e, m] * inverse
            if own:
                headed = head_in[e, m].astype(F32)
                sums[2] += grad * normed
                sums[3] += headed * pull0
                sums[4] += headed * pull1
            grad = norm_back(grad * gains[2], normed, inverse)
            stream_grad[e, m] = grad
            grads1[e, m] = (grad * (slope1[e, m] * inside(e))).astype(BF16)

    def tap_grads(b, rows, fresh):
        grads, inputs = ((grads0, inputs0), (grads1, inputs1))[b]
        shifted, windows = [], []
        for e in rows:
            for m in range(HERE):
                grad = grads[e, m]
                shifted.append(jnp.concatenate([from_right(grad), grad, from_left(grad)], axis=0))
                windows.append(inputs[pl.ds(e - 1, 3), m].reshape(3 * CH, COLS))
        found = dot_rows(jnp.concatenate(shifted, axis=1), jnp.concatenate(windows, axis=1))
        at = pl.ds(0, 3 * CH)
        tap_sum[b, :, at] = found if fresh else tap_sum[b, :, at] + found

    def backward(b, e, last):
        source, stream, inverses = ((grads0, stream0, inverse0), (grads1, stream1, inverse1))[b]
        for m in range(HERE):
            window = source[pl.ds(e - 1, 4), m].reshape(4 * CH, COLS)
            taken = dot(backward_taps[b], window)
            for ro in range(2):
                left, middle, right = [taken[(2 * dc + ro) * CH : (2 * dc + ro + 1) * CH] for dc in range(3)]
                grad = middle + from_right(left) + from_left(right)
                inverse = inverses[e + ro, m, pl.ds(0, 1), :]
                normed = stream[e + ro, m] * inverse
                counted = HALO <= e + ro < HALO + ROWS
                if counted:
                    sums[b] += grad * normed
                total = stream_grad[e + ro, m] + norm_back(grad * gains[b], normed, inverse)
                if b == 1:
                    stream_grad[e + ro, m] = total
                    grads0[e + ro, m] = (total * (slope0[e + ro, m] * inside(e + ro))).astype(BF16)
                else:
                    last(e + ro, m, total.astype(BF16))

    def to_parts(b):
        for at in range(GROUP):
            parts[b, at] = tap_sum[b, pl.ds(CHUNK * (at // 2), CHUNK), pl.ds(128 * (at % 2), 128)]

    def scatter(b):
        return [
            send(parts.at[b, rank], scattered.at[b, step], plane_sems.at[b], step, device)
            for step, (device, rank) in enumerate(groups[b][0])
        ]

    def spread_out(b):
        in_first, in_second = ranks[b]
        total = parts[b, in_first]
        for step in range(GROUP - 1):
            total = total + scattered[b, step]
        spread[b, in_second] = total
        return [
            send(spread.at[b, in_second], spread.at[b, in_second], line_sems.at[b], step, device)
            for step, (device, _) in enumerate(groups[b][1])
        ]

    def gather(b):
        total = spread[b, 0]
        for rank in range(1, GROUP):
            total = total + spread[b, rank]
        in_first = ranks[b][0]
        gathered[b, in_first] = total
        return [
            send(gathered.at[b, in_first], gathered.at[b, in_first], back_sems.at[b], step, device)
            for step, (device, _) in enumerate(groups[b][0])
        ]

    wait(own_copies)
    loss_tile = jnp.zeros((8, COLS), F32)
    for m in range(HERE):
        loss_tile += pull_apart(m, (0, 1), weight_tiles[0])
    over_rows(HALO, ROWS, lambda e: top(e, True))
    tap_grads(1, range(HALO, HALO + ROWS), True)
    to_parts(1)
    first_1 = scatter(1)
    over(5, 3, lambda e: backward(1, e, None))
    tap_grads(0, range(5, 11), True)
    wait(edge_copies)
    for m in range(HERE):
        pull_apart(m, (2,), weight_tiles[1])
    for e in (2, 3, 12, 13):
        top(e, False)
    for e in (3, 11):
        backward(1, e, None)
    tap_grads(0, (4, 11), False)
    to_parts(0)
    first_0 = scatter(0)
    wait(first_1)
    second_1 = spread_out(1)

    small[...] = jnp.zeros_like(small)
    sum_noise = tap_sum.at[0, pl.ds(0, CH), pl.ds(0, NOISE)]
    sum_noise[...] = jnp.zeros((CH, NOISE), F32)

    def last(e, m, entry_grad):
        sum_noise[...] += dot_rows(entry_grad, noise[e, m].astype(BF16))

    over(4, 4, lambda e: backward(0, e, last))
    column = lax.broadcasted_iota(jnp.int32, (CH, NOISE), 1)
    late = sum_noise[...]
    for at in range(5):
        small[pl.ds(at, 1), pl.ds(0, CH)] = as_row(jnp.sum(sums[at], axis=1, keepdims=True))
    for k in range(NOISE):
        picked = jnp.sum(jnp.where(column == k, late, 0.0), axis=1, keepdims=True)
        small[pl.ds(5 + k, 1), pl.ds(0, CH)] = as_row(picked)
    loss = jnp.sum(jnp.sum(loss_tile, axis=0, keepdims=True), axis=1, keepdims=True) * (1.0 / cells)
    small[pl.ds(13, 1), :] = jnp.broadcast_to(loss, (1, 128))
    small_in[in_plane] = small[...]
    small_1 = [
        send(small, small_in.at[in_plane], small_sems, step, device) for step, (device, _) in enumerate(plane)
    ]
    wait(first_0)
    second_0 = spread_out(0)
    wait(second_1)
    back_1 = gather(1)
    wait(small_1)
    total = small_in[0]
    for rank in range(1, GROUP):
        total = total + small_in[rank]
    small_line[in_line] = total
    small_2 = [
        send(small_line.at[in_line], small_line.at[in_line], small_line_sems, step, device)
        for step, (device, _) in enumerate(line)
    ]
    wait(second_0)
    back_0 = gather(0)
    wait(back_1)
    wait(small_2)
    total = small_line[0]
    for rank in range(1, GROUP):
        total = total + small_line[rank]
    small_out[...] = total
    wait(back_0)


def unpack_kernel(
    predictions, gathered, small, loss, pred_out, grad_conv, grad_gain, grad_head, grad_head_gain, grad_noise, whole
):
    pred_out[...] = predictions[...]
    for b in range(2):
        for at in range(GROUP):
            whole[pl.ds(CHUNK * (at // 2), CHUNK), pl.ds(128 * (at % 2), 128)] = gathered[b, at]
        for dr in range(3):
            for dc in range(3):
                grad_conv[b, 3 * dr + dc] = whole[pl.ds(CH * dc, CH), pl.ds(CH * dr, CH)]
    for out, first, count in ((grad_gain, 0, 2), (grad_head_gain, 2, 1), (grad_head, 3, 2), (grad_noise, 5, NOISE)):
        out[...] = small[pl.ds(first, count), pl.ds(0, CH)]
    loss[...] = small[pl.ds(13, 1), pl.ds(0, 1)]


def on_device(
    block_input,
    member_seeds,
    targets,
    land_mask,
    noise_weight,
    conv_weight,
    block_gain,
    head_weight,
    head_gain,
):
    vmem = pl.BlockSpec(memory_space=pltpu.VMEM)
    far = pl.BlockSpec(memory_space=pltpu.HBM)

    def field(*shape):
        return pltpu.VMEM((EXT, HERE) + shape, F32)

    def half(*shape):
        return pltpu.VMEM((EXT, HERE) + shape, BF16)

    def sems(*shape):
        return pltpu.SemaphoreType.DMA(shape)

    scratch = dict(
        block_input=pltpu.VMEM(block_input.shape, BF16),
        seeds=pltpu.SMEM(member_seeds.shape, jnp.int32),
        targets=pltpu.VMEM(targets.shape, F32),
        land_mask=pltpu.VMEM(land_mask.shape, jnp.int32),
        noise_weight=pltpu.VMEM((NOISE, CH), BF16),
        conv_weight=pltpu.VMEM(conv_weight.shape, BF16),
        block_gain=pltpu.VMEM(block_gain.shape, F32),
        head_weight=pltpu.VMEM(head_weight.shape, BF16),
        head_gain=pltpu.VMEM((1, CH), F32),
        load_sems=sems(9),
        turned=pltpu.VMEM((HERE, 2, CH * ROWS, 128), F32),
        raw=half(CH, COLS),
        noise=field(NOISE, COLS),
        stream0=field(CH, COLS),
        stream1=field(CH, COLS),
        stream2=field(CH, COLS),
        inverse0=field(8, COLS),
        inverse1=field(8, COLS),
        inverse2=field(8, COLS),
        slope0=field(CH, COLS),
        slope1=field(CH, COLS),
        inputs0=half(CH, COLS),
        inputs1=half(CH, COLS),
        grads0=half(CH, COLS),
        grads1=half(CH, COLS),
        stream_grad=field(CH, COLS),
        head_in=half(CH, COLS),
        forward_taps=pltpu.VMEM((2, 6 * CH, 4 * CH), BF16),
        backward_taps=pltpu.VMEM((2, 6 * CH, 4 * CH), BF16),
        noise_taps=pltpu.VMEM((CH, NOISE), BF16),
        gains=pltpu.VMEM((5, CH, COLS), F32),
        edge_out=pltpu.VMEM((2, 8, COLS), F32),
        edge_in=pltpu.VMEM((2, 8, COLS), F32),
        target_tiles=pltpu.VMEM((3, 8, COLS), F32),
        weight_tiles=pltpu.VMEM((2, 8, COLS), F32),
        own_pred=pltpu.VMEM((3, HERE, 8, COLS), F32),
        all_pred=pltpu.VMEM((MEMS, 3, HERE, 8, COLS), F32),
        pred_grad=pltpu.VMEM((3, HERE, 8, COLS), F32),
        sums=pltpu.VMEM((5, CH, COLS), F32),
        tap_sum=pltpu.VMEM((2, 3 * CH, 256), F32),
        parts=pltpu.VMEM((2, GROUP, CHUNK, 128), F32),
        scattered=pltpu.VMEM((2, GROUP - 1, CHUNK, 128), F32),
        spread=pltpu.VMEM((2, GROUP, CHUNK, 128), F32),
        small=pltpu.VMEM((16, 128), F32),
        small_in=pltpu.VMEM((GROUP, 16, 128), F32),
        small_line=pltpu.VMEM((GROUP, 16, 128), F32),
        halo_sems=sems(2, 6),
        mem_sems=sems(2, 2, MEMS - 1),
        plane_sems=sems(2, 2, GROUP - 1),
        line_sems=sems(2, 2, GROUP - 1),
        back_sems=sems(2, 2, GROUP - 1),
        small_sems=sems(2, GROUP - 1),
        small_line_sems=sems(2, GROUP - 1),
    )
    predictions, gathered, small = pl.pallas_call(
        step_kernel,
        out_shape=(
            jax.ShapeDtypeStruct((HERE, 2, ROWS, COLS), F32),
            jax.ShapeDtypeStruct((2, GROUP, CHUNK, 128), F32),
            jax.ShapeDtypeStruct((16, 128), F32),
        ),
        in_specs=[far] * 9,
        out_specs=(vmem, vmem, vmem),
        scratch_shapes=list(scratch.values()),
        compiler_params=pltpu.CompilerParams(
            collective_id=0, has_side_effects=True, vmem_limit_bytes=VMEM_BYTES
        ),
        name="train_step",
    )(
        block_input,
        member_seeds,
        targets,
        land_mask,
        noise_weight.T,
        conv_weight,
        block_gain,
        head_weight,
        head_gain.reshape(1, CH),
    )
    loss, predictions, grad_conv, grad_block_gain, grad_head_weight, grad_head_gain, grad_noise = pl.pallas_call(
        unpack_kernel,
        out_shape=(
            jax.ShapeDtypeStruct((1, 1), F32),
            jax.ShapeDtypeStruct((HERE, 2, ROWS, COLS), F32),
            jax.ShapeDtypeStruct((2, 9, CH, CH), F32),
            jax.ShapeDtypeStruct((2, CH), F32),
            jax.ShapeDtypeStruct((2, CH), F32),
            jax.ShapeDtypeStruct((1, CH), F32),
            jax.ShapeDtypeStruct((NOISE, CH), F32),
        ),
        in_specs=[vmem] * 3,
        out_specs=(vmem,) * 7,
        scratch_shapes=[pltpu.VMEM((3 * CH, 256), F32)],
        compiler_params=pltpu.CompilerParams(vmem_limit_bytes=VMEM_BYTES),
        name="unpack",
    )(predictions, gathered, small)
    return (
        loss.reshape(()),
        predictions,
        grad_conv,
        grad_block_gain,
        grad_head_weight,
        grad_head_gain.reshape(CH),
        grad_noise.T,
    )


def solution(mesh):
    return jax.shard_map(
        on_device,
        mesh=mesh,
        in_specs=(
            P("mem", None, "tile", None),
            P("mem"),
            P(None, "tile", None),
            P("tile", None),
            P(),
            P(),
            P(),
            P(),
            P(),
        ),
        out_specs=(P(), P("mem", None, "tile", None), P(), P(), P(), P(), P()),
        check_vma=False,
    )
```

```python
import jax
import jax.numpy as jnp
from jax import lax
from jax.experimental import pallas as pl
from jax.experimental.pallas import tpu as pltpu
from jax.sharding import PartitionSpec as P

LOSS_SCALE = 16384
MESH_ID = pl.DeviceIdType.MESH
GROUP = 16
MEMS = 8
TILES = 32
HERE = 2
MEMBERS = 16
ROWS = 8
COLS = 256
CH = 64
NOISE = 8
HALO = 4
EXT = ROWS + 2 * HALO
GRID_ROWS = ROWS * TILES
PART = 6
DEPTH = 8
VMEM_BYTES = 63 * 2**20
F32 = jnp.float32
BF16 = jnp.bfloat16
eps_norm = 1e-05
smooth_sq = 0.01


def coordinates():
    mem, tile = lax.axis_index("mem"), lax.axis_index("tile")
    return mem // 2, (tile // 2) % 4, (tile // 8) * 2 + mem % 2, tile % 2


def device_at(x, y, z, core):
    return (x * 2 + z % 2, (z // 2) * 8 + y * 2 + core)


def plane_rank():
    x, y, _, _ = coordinates()
    return x * 4 + y


def plane_device(rank):
    _, _, z, core = coordinates()
    return device_at(rank // 4, rank % 4, z, core)


def depth_device(rank):
    x, y, _, core = coordinates()
    return device_at(x, y, rank, core)


def core_device(rank):
    x, y, z, _ = coordinates()
    return device_at(x, y, z, rank)


def mem_device(rank):
    return (rank, lax.axis_index("tile"))


def others(rank, count):
    return [lax.rem(rank + step, count) for step in range(1, count)]


def modulo(value, base):
    quotient = jnp.floor(value.astype(F32) * (1.0 / base)).astype(jnp.int32)
    rest = value - quotient * base
    rest = jnp.where(rest < 0, rest + base, rest)
    return jnp.where(rest >= base, rest - base, rest)


def noise_row(seed, row):
    channel = lax.broadcasted_iota(jnp.int32, (NOISE, COLS), 0)
    column = lax.broadcasted_iota(jnp.int32, (NOISE, COLS), 1)
    first = modulo(7919 * channel + column + (seed + row * COLS), 65521)
    second = modulo(first * 3001 + 12345, 65521)
    folded = modulo(second, 46337)
    third = modulo(folded * folded + second, 65521)
    fourth = modulo(third * 2897 + 4111, 65521)
    return ((fourth - 32760).astype(F32) / 18914.0).astype(BF16)


def columns_of(shape):
    return lax.broadcasted_iota(jnp.int32, shape, len(shape) - 1)


def from_left(value):
    return jnp.where(columns_of(value.shape) == 0, jnp.zeros((), value.dtype), pltpu.roll(value, 1, axis=1))


def from_right(value):
    return jnp.where(
        columns_of(value.shape) == COLS - 1, jnp.zeros((), value.dtype), pltpu.roll(value, COLS - 1, axis=1)
    )


def dot(left, right):
    return jnp.dot(left, right, preferred_element_type=F32)


def dot_rows(left, right):
    return lax.dot_general(left, right, (((1,), (1,)), ((), ())), preferred_element_type=F32)


def diagonal():
    shape = (CH, CH)
    return lax.broadcasted_iota(jnp.int32, shape, 0) == lax.broadcasted_iota(jnp.int32, shape, 1)


def as_column(row):
    return jnp.sum(jnp.where(diagonal(), jnp.broadcast_to(row, (CH, CH)), 0.0), axis=1, keepdims=True)


def as_row(column):
    return jnp.sum(jnp.where(diagonal(), jnp.broadcast_to(column, (CH, CH)), 0.0), axis=0, keepdims=True)


def silu_parts(value):
    gate = 0.5 * jnp.tanh(0.5 * value) + 0.5
    gated = value * gate
    return gated, gate + gated * (1.0 - gate)


def inverse_scale(stream):
    return lax.rsqrt(jnp.sum(stream * stream, axis=0, keepdims=True) * (1.0 / CH) + eps_norm)


def norm_back(grad, normed, inverse):
    mean = jnp.sum(grad * normed, axis=0, keepdims=True) * (1.0 / CH)
    return (grad - normed * mean) * inverse


def step_kernel(
    block_input_far,
    seeds_far,
    targets_far,
    land_mask_far,
    noise_weight_far,
    conv_weight_far,
    block_gain_far,
    head_weight_far,
    head_gain_far,
    predictions,
    gathered,
    small_out,
    block_input,
    seeds,
    targets,
    land_mask,
    noise_weight,
    conv_weight,
    block_gain,
    head_weight,
    head_gain,
    load_sems,
    turned,
    raw,
    noise,
    stream0,
    stream1,
    stream2,
    inverse0,
    inverse1,
    inverse2,
    slope0,
    slope1,
    inputs0,
    inputs1,
    grads0,
    grads1,
    stream_grad,
    head_in,
    forward_taps,
    backward_taps,
    noise_taps,
    gains,
    edge_out,
    edge_in,
    target_tiles,
    weight_tiles,
    own_pred,
    all_pred,
    pred_grad,
    sums,
    tap_sum,
    parts,
    core_in,
    scattered,
    spread,
    small,
    small_core,
    small_in,
    small_line,
    halo_sems,
    mem_sems,
    core_sems,
    plane_sems,
    line_sems,
    back_sems,
    small_sems,
    small_line_sems,
):
    mem, tile = lax.axis_index("mem"), lax.axis_index("tile")
    in_plane = plane_rank()
    _, _, depth, core = coordinates()
    other_core = 1 - core
    below, above = lax.rem(tile + 1, TILES), lax.rem(tile + TILES - 1, TILES)
    plane = [(plane_device(rank), rank) for rank in others(in_plane, GROUP)]
    line = [(depth_device(rank), rank) for rank in others(depth, DEPTH)]
    members = [(mem_device(rank), rank) for rank in others(mem, MEMS)]

    loads = [
        pltpu.make_async_copy(far, near, load_sems.at[at])
        for at, (far, near) in enumerate(
            (
                (block_input_far, block_input),
                (seeds_far, seeds),
                (targets_far, targets),
                (land_mask_far, land_mask),
                (noise_weight_far, noise_weight),
                (conv_weight_far, conv_weight),
                (block_gain_far, block_gain),
                (head_weight_far, head_weight),
                (head_gain_far, head_gain),
            )
        )
    ]
    for load in loads:
        load.start()

    barrier = pltpu.get_barrier_semaphore()
    for device in [(mem, below), (mem, above)] + [core_device(other_core)] + [
        d for d, _ in plane + line + members
    ]:
        pl.semaphore_signal(barrier, inc=1, device_id=device, device_id_type=MESH_ID)

    def send(source, target, sems, slot, device):
        copy = pltpu.make_async_remote_copy(
            src_ref=source,
            dst_ref=target,
            send_sem=sems.at[0, slot],
            recv_sem=sems.at[1, slot],
            device_id=device,
            device_id_type=MESH_ID,
        )
        copy.start()
        return copy

    def wait(copies):
        for copy in copies:
            copy.wait()

    loads[0].wait()
    for m in range(HERE):
        for half in range(2):
            lanes = pl.ds(128 * half, 128)
            turned[m, half] = block_input[m, :, :, lanes].astype(F32).reshape(CH * ROWS, 128)

    def bring(rows):
        for r in rows:
            for m in range(HERE):
                for half in range(2):
                    lanes = pl.ds(128 * half, 128)
                    raw[HALO + r, m, :, lanes] = turned[m, half, pl.ds(r, CH, stride=ROWS), :].astype(BF16)

    bring((0, 1, 6, 7))
    pl.semaphore_wait(barrier, 3 + (GROUP - 1) + (DEPTH - 1) + (MEMS - 1))

    def halo(up, down, up_to, down_to, slot):
        return [
            send(raw.at[pl.ds(up, 2)], raw.at[pl.ds(up_to, 2)], halo_sems, slot, (mem, above)),
            send(raw.at[pl.ds(down, 2)], raw.at[pl.ds(down_to, 2)], halo_sems, slot + 1, (mem, below)),
        ]

    near_copies = halo(4, 10, 12, 2, 0)
    bring(range(2, 6))
    far_copies = halo(6, 8, 14, 0, 2)
    wait(loads[1:])
    for side, start in ((0, 0), (1, ROWS - 2)):
        edge_out[side] = jnp.zeros((8, COLS), F32)
        for v in range(2):
            edge_out[side, pl.ds(2 * v, 2), :] = targets[v, pl.ds(start, 2), :]
        edge_out[side, pl.ds(4, 2), :] = land_mask[pl.ds(start, 2), :].astype(F32)
    far_copies += [
        send(edge_out.at[0], edge_in.at[1], halo_sems, 4, (mem, above)),
        send(edge_out.at[1], edge_in.at[0], halo_sems, 5, (mem, below)),
    ]

    unit = diagonal().astype(F32).astype(BF16)
    blank = jnp.zeros((CH, CH), BF16)
    for b in range(2):
        for dc in range(3):
            taps = [conv_weight[b, 3 * dr + dc] for dr in range(3)]
            turned_taps = [dot_rows(unit, tap).astype(BF16) for tap in taps]
            for ro in range(2):
                at = pl.ds((2 * dc + ro) * CH, CH)
                ahead = [blank] * ro + turned_taps + [blank] * (1 - ro)
                forward_taps[b, at, :] = dot_rows(unit, jnp.concatenate(ahead, axis=0)).astype(BF16)
                back = [blank] * ro + taps[::-1] + [blank] * (1 - ro)
                backward_taps[b, at, :] = dot_rows(unit, jnp.concatenate(back, axis=0)).astype(BF16)
    noise_taps[...] = dot_rows(unit, noise_weight[...]).astype(BF16)
    columns = [block_gain[pl.ds(0, 1), :], block_gain[pl.ds(1, 1), :], head_gain[...]]
    columns += [head_weight[pl.ds(v, 1), :].astype(F32) for v in range(2)]
    for at, row in enumerate(columns):
        gains[at] = jnp.broadcast_to(as_column(row), (CH, COLS))
    for at in range(5):
        sums[at] = jnp.zeros((CH, COLS), F32)
    tap_sum[...] = jnp.zeros_like(tap_sum)
    parts[...] = jnp.zeros_like(parts)

    def inside(e):
        row = tile * ROWS - HALO + e
        return jnp.where((row >= 0) & (row < GRID_ROWS), 1.0, 0.0).astype(F32)

    def make_noise(e):
        row = jnp.clip(tile * ROWS - HALO + e, 0, GRID_ROWS - 1)
        for m in range(HERE):
            noise[e, m] = noise_row(seeds[m], row).astype(F32)

    def entry(e):
        for m in range(HERE):
            stream = raw[e, m].astype(F32) + dot(noise_taps[...], noise[e, m].astype(BF16))
            stream0[e, m] = stream
            inverse = inverse_scale(stream)
            inverse0[e, m] = jnp.broadcast_to(inverse, (8, COLS))
            inputs0[e, m] = (stream * (inverse * inside(e)) * gains[0]).astype(BF16)

    def forward(b, e, ms=range(HERE)):
        source, stream_in, stream_out, slope = (
            (inputs0, stream0, stream1, slope0),
            (inputs1, stream1, stream2, slope1),
        )[b]
        for m in ms:
            window = source[pl.ds(e - 1, 4), m].reshape(4 * CH, COLS)
            taken = dot(forward_taps[b], window)
            for ro in range(2):
                left, middle, right = [taken[(2 * dc + ro) * CH : (2 * dc + ro + 1) * CH] for dc in range(3)]
                gated, bent = silu_parts(middle + from_left(left) + from_right(right))
                slope[e + ro, m] = bent
                stream = stream_in[e + ro, m] + gated
                stream_out[e + ro, m] = stream
                inverse = inverse_scale(stream)
                if b == 0:
                    inverse1[e + ro, m] = jnp.broadcast_to(inverse, (8, COLS))
                    inputs1[e + ro, m] = (stream * (inverse * inside(e + ro)) * gains[1]).astype(BF16)
                else:
                    inverse2[e + ro, m] = jnp.broadcast_to(inverse, (8, COLS))
                    headed = (stream * inverse * gains[2]).astype(BF16)
                    head_in[e + ro, m] = headed
                    found = dot(head_weight[...], headed)
                    place(own_pred, m, e + ro, found)

    def spots(e):
        if 6 <= e < 10:
            return [(0, e - 6), (0, e - 2)]
        part = 1 if HALO <= e < HALO + ROWS else 2
        at = e - HALO + 2 * part - 2 if e < 8 else e - HALO - ROWS + 6 - 2 * part
        return [(part, at), (part, at + 4)]

    def place(ref, m, e, pair):
        for v, (part, at) in enumerate(spots(e)):
            ref[part, m, pl.ds(at, 1), :] = pair[v : v + 1]

    def over(first, count, body):
        for i in range(count):
            body(first + 2 * i)

    def over_rows(first, count, body):
        for i in range(count):
            body(first + i)

    def share(part):
        all_pred[mem, part] = own_pred[part]
        return [
            send(own_pred.at[part], all_pred.at[mem, part], mem_sems.at[part], step, device)
            for step, (device, _) in enumerate(members)
        ]

    over_rows(HALO, ROWS, make_noise)
    over_rows(HALO, ROWS, entry)
    over(5, 3, lambda e: forward(0, e))
    over(6, 2, lambda e: forward(1, e))
    shared = [share(0)]
    over_rows(0, HALO, make_noise)
    over_rows(HALO + ROWS, HALO, make_noise)
    for v in range(2):
        target_tiles[0, pl.ds(4 * v, 4), :] = targets[v, pl.ds(2, 4), :]
        weight_tiles[0, pl.ds(4 * v, 4), :] = land_mask[pl.ds(2, 4), :].astype(F32)
        for side in range(2):
            at = pl.ds(4 * v + 2 * side, 2)
            target_tiles[1, at, :] = targets[v, pl.ds(6 * side, 2), :]
            weight_tiles[1, at, :] = land_mask[pl.ds(6 * side, 2), :].astype(F32)
    wait(near_copies)
    for e in (2, 3, 12, 13):
        entry(e)
    for b, e in ((0, 3), (0, 11), (1, 4), (1, 10)):
        forward(b, e)
    shared.append(share(1))
    wait(far_copies)
    for e in (0, 1, 14, 15):
        entry(e)
    for b, e in ((0, 1), (0, 13), (1, 2), (1, 12)):
        forward(b, e)
    shared.append(share(2))
    for v in range(2):
        for m in range(HERE):
            predictions[m, v, pl.ds(2, 4), :] = own_pred[0, m, pl.ds(4 * v, 4), :]
            for side in range(2):
                predictions[m, v, pl.ds(6 * side, 2), :] = own_pred[1, m, pl.ds(4 * v + 2 * side, 2), :]
        for side in range(2):
            at = pl.ds(4 * v + 2 * side, 2)
            target_tiles[2, at, :] = edge_in[side, pl.ds(2 * v, 2), :]
            weight_tiles[2, at, :] = edge_in[side, pl.ds(4, 2), :]
    place_in = lax.broadcasted_iota(jnp.int32, (8, COLS), 0) % 4
    for part, (first, second) in enumerate(((2, 4), (0, 6), (-2, 8))):
        rows = jnp.where(place_in < 2, place_in + first, place_in - 2 + second)
        area = 1.0 - 2.0 * (rows + tile * ROWS).astype(F32) / (3.0 * GRID_ROWS)
        weight_tiles[part] = area * (1.0 + weight_tiles[part])

    cells = GRID_ROWS * COLS

    def length_sq(gap):
        square = gap * gap
        return square + pltpu.roll(square, 4, axis=0) + smooth_sq

    def pull_apart(m, part):
        mine = own_pred[part, m]
        pull = jnp.zeros((8, COLS), F32)
        total = jnp.zeros((8, COLS), F32) - smooth_sq**0.5
        for n in range(MEMBERS):
            gap = mine - all_pred[n // HERE, part, n % HERE]
            square = length_sq(gap)
            inverse = lax.rsqrt(square)
            pull = pull + gap * inverse
            total = total + square * inverse
        miss = mine - target_tiles[part]
        square = length_sq(miss)
        inverse = lax.rsqrt(square)
        weights = weight_tiles[part]
        grad = (weights * (LOSS_SCALE / cells)) * (
            miss * inverse * (1.0 / MEMBERS) - pull * (1.0 / (MEMBERS * (MEMBERS - 1.0)))
        )
        pred_grad[part, m] = grad.astype(BF16).astype(F32)
        return weights * (
            square * inverse * (1.0 / MEMBERS) - total * (1.0 / (2.0 * MEMBERS * (MEMBERS - 1)))
        )

    def top(e, own):
        for m in range(HERE):
            (part0, at0), (part1, at1) = spots(e)
            pull0 = pred_grad[part0, m, pl.ds(at0, 1), :]
            pull1 = pred_grad[part1, m, pl.ds(at1, 1), :]
            grad = gains[3] * pull0 + gains[4] * pull1
            inverse = inverse2[e, m, pl.ds(0, 1), :]
            normed = stream2[e, m] * inverse
            if own:
                headed = head_in[e, m].astype(F32)
                sums[2] += grad * normed
                sums[3] += headed * pull0
                sums[4] += headed * pull1
            grad = norm_back(grad * gains[2], normed, inverse)
            stream_grad[e, m] = grad
            grads1[e, m] = (grad * (slope1[e, m] * inside(e))).astype(BF16)

    def tap_grads(b, rows, fresh):
        grads, inputs = ((grads0, inputs0), (grads1, inputs1))[b]
        shifted, windows = [], []
        for e in rows:
            for m in range(HERE):
                grad = grads[e, m]
                shifted.append(jnp.concatenate([from_right(grad), grad, from_left(grad)], axis=0))
                windows.append(inputs[pl.ds(e - 1, 3), m].reshape(3 * CH, COLS))
        found = dot_rows(jnp.concatenate(shifted, axis=1), jnp.concatenate(windows, axis=1))
        at = pl.ds(0, 3 * CH)
        tap_sum[b, :, at] = found if fresh else tap_sum[b, :, at] + found

    def backward(b, e, last):
        source, stream, inverses = ((grads0, stream0, inverse0), (grads1, stream1, inverse1))[b]
        for m in range(HERE):
            window = source[pl.ds(e - 1, 4), m].reshape(4 * CH, COLS)
            taken = dot(backward_taps[b], window)
            for ro in range(2):
                left, middle, right = [taken[(2 * dc + ro) * CH : (2 * dc + ro + 1) * CH] for dc in range(3)]
                grad = middle + from_right(left) + from_left(right)
                inverse = inverses[e + ro, m, pl.ds(0, 1), :]
                normed = stream[e + ro, m] * inverse
                counted = HALO <= e + ro < HALO + ROWS
                if counted:
                    sums[b] += grad * normed
                total = stream_grad[e + ro, m] + norm_back(grad * gains[b], normed, inverse)
                if b == 1:
                    stream_grad[e + ro, m] = total
                    grads0[e + ro, m] = (total * (slope0[e + ro, m] * inside(e + ro))).astype(BF16)
                else:
                    last(e + ro, m, total.astype(BF16))

    def across(source, target, sems, slot):
        return [send(source, target, sems, slot, core_device(other_core))]

    def to_core(b):
        for half in range(2):
            for at in range(GROUP):
                rows = pl.ds(PART * (GROUP * half + at), PART)
                parts[b, half, at, pl.ds(0, PART), :] = tap_sum[b, rows, :]
        return across(parts.at[b, other_core], core_in.at[b], core_sems, b)

    def to_plane(b):
        parts[b, core] = parts[b, core] + core_in[b]
        return [
            send(parts.at[b, core, rank], scattered.at[b, step], plane_sems.at[b], step, device)
            for step, (device, rank) in enumerate(plane)
        ]

    def to_depth(b):
        total = parts[b, core, in_plane]
        for step in range(GROUP - 1):
            total = total + scattered[b, step]
        spread[b, depth] = total
        return [
            send(spread.at[b, depth], spread.at[b, depth], line_sems.at[b], step, device)
            for step, (device, _) in enumerate(line)
        ]

    def to_plane_again(b):
        total = spread[b, 0]
        for rank in range(1, DEPTH):
            total = total + spread[b, rank]
        gathered[b, core, in_plane] = total
        mine = gathered.at[b, core, in_plane]
        return [send(mine, mine, back_sems.at[b], step, device) for step, (device, _) in enumerate(plane)]

    def to_core_again(b):
        return across(gathered.at[b, core], gathered.at[b, core], core_sems, 2 + b)

    def grads_of(part):
        found = jnp.zeros((8, COLS), F32)
        for m in range(HERE):
            found += pull_apart(m, part)
        return found

    wait(shared[0])
    loss_tile = grads_of(0)
    over_rows(6, 4, lambda e: top(e, True))
    tap_grads(1, range(6, 10), True)
    backward(1, 7, None)
    wait(shared[1])
    loss_tile += grads_of(1)
    for e in (4, 5, 10, 11):
        top(e, True)
    tap_grads(1, (4, 5, 10, 11), False)
    core_1 = to_core(1)
    backward(1, 5, None)
    backward(1, 9, None)
    wait(core_1)
    plane_1 = to_plane(1)
    tap_grads(0, range(5, 11), True)
    wait(shared[2])
    grads_of(2)
    for e in (2, 3, 12, 13):
        top(e, False)
    for e in (3, 11):
        backward(1, e, None)
    tap_grads(0, (4, 11), False)
    core_0 = to_core(0)

    small[...] = jnp.zeros_like(small)
    sum_noise = tap_sum.at[0, pl.ds(0, CH), pl.ds(0, NOISE)]
    sum_noise[...] = jnp.zeros((CH, NOISE), F32)

    def last(e, m, entry_grad):
        sum_noise[...] += dot_rows(entry_grad, noise[e, m].astype(BF16))

    over(4, 2, lambda e: backward(0, e, last))
    wait(core_0)
    plane_0 = to_plane(0)
    over(8, 2, lambda e: backward(0, e, last))
    column = lax.broadcasted_iota(jnp.int32, (CH, NOISE), 1)
    late = sum_noise[...]
    rows = [as_row(jnp.sum(sums[at], axis=1, keepdims=True)) for at in range(5)]
    for k in range(NOISE):
        rows.append(as_row(jnp.sum(jnp.where(column == k, late, 0.0), axis=1, keepdims=True)))
    loss = jnp.sum(jnp.sum(loss_tile, axis=0, keepdims=True), axis=1, keepdims=True) * (0.5 / cells)
    rows.append(jnp.broadcast_to(loss, (1, CH)))
    for at, row in enumerate(rows):
        small[pl.ds(at // 2, 1), pl.ds(CH * (at % 2), CH)] = row
    small_0 = across(small, small_core, core_sems, 4)
    wait(plane_1)
    depth_1 = to_depth(1)
    wait(small_0)
    small_in[in_plane] = small[...] + small_core[...]
    mine = small_in.at[in_plane]
    small_1 = [send(mine, mine, small_sems, step, device) for step, (device, _) in enumerate(plane)]
    wait(plane_0)
    depth_0 = to_depth(0)
    wait(depth_1)
    back_1 = to_plane_again(1)
    wait(small_1)
    total = small_in[0]
    for rank in range(1, GROUP):
        total = total + small_in[rank]
    small_line[depth] = total
    mine = small_line.at[depth]
    small_2 = [send(mine, mine, small_line_sems, step, device) for step, (device, _) in enumerate(line)]
    wait(depth_0)
    back_0 = to_plane_again(0)
    wait(back_1)
    last_1 = to_core_again(1)
    wait(small_2)
    total = small_line[0]
    for rank in range(1, DEPTH):
        total = total + small_line[rank]
    small_out[...] = total
    wait(back_0)
    last_0 = to_core_again(0)
    wait(last_1 + last_0)


def unpack_kernel(
    predictions, gathered, small, loss, pred_out, grad_conv, grad_gain, grad_head, grad_head_gain, grad_noise, whole
):
    pred_out[...] = predictions[...]
    for b in range(2):
        for half in range(2):
            for at in range(GROUP):
                whole[pl.ds(PART * (GROUP * half + at), PART), :] = gathered[b, half, at, pl.ds(0, PART), :]
        for dr in range(3):
            for dc in range(3):
                grad_conv[b, 3 * dr + dc] = whole[pl.ds(CH * dc, CH), pl.ds(CH * dr, CH)]
    for out, first, count in ((grad_gain, 0, 2), (grad_head_gain, 2, 1), (grad_head, 3, 2), (grad_noise, 5, NOISE)):
        for at in range(count):
            out[pl.ds(at, 1), :] = small[pl.ds((first + at) // 2, 1), pl.ds(CH * ((first + at) % 2), CH)]
    loss[...] = small[pl.ds(6, 1), pl.ds(CH, 1)]


def on_device(
    block_input,
    member_seeds,
    targets,
    land_mask,
    noise_weight,
    conv_weight,
    block_gain,
    head_weight,
    head_gain,
):
    vmem = pl.BlockSpec(memory_space=pltpu.VMEM)
    far = pl.BlockSpec(memory_space=pltpu.HBM)

    def field(*shape):
        return pltpu.VMEM((EXT, HERE) + shape, F32)

    def half(*shape):
        return pltpu.VMEM((EXT, HERE) + shape, BF16)

    def sems(*shape):
        return pltpu.SemaphoreType.DMA(shape)

    scratch = dict(
        block_input=pltpu.VMEM(block_input.shape, BF16),
        seeds=pltpu.SMEM(member_seeds.shape, jnp.int32),
        targets=pltpu.VMEM(targets.shape, F32),
        land_mask=pltpu.VMEM(land_mask.shape, jnp.int32),
        noise_weight=pltpu.VMEM((NOISE, CH), BF16),
        conv_weight=pltpu.VMEM(conv_weight.shape, BF16),
        block_gain=pltpu.VMEM(block_gain.shape, F32),
        head_weight=pltpu.VMEM(head_weight.shape, BF16),
        head_gain=pltpu.VMEM((1, CH), F32),
        load_sems=sems(9),
        turned=pltpu.VMEM((HERE, 2, CH * ROWS, 128), F32),
        raw=half(CH, COLS),
        noise=field(NOISE, COLS),
        stream0=field(CH, COLS),
        stream1=field(CH, COLS),
        stream2=field(CH, COLS),
        inverse0=field(8, COLS),
        inverse1=field(8, COLS),
        inverse2=field(8, COLS),
        slope0=field(CH, COLS),
        slope1=field(CH, COLS),
        inputs0=half(CH, COLS),
        inputs1=half(CH, COLS),
        grads0=half(CH, COLS),
        grads1=half(CH, COLS),
        stream_grad=field(CH, COLS),
        head_in=half(CH, COLS),
        forward_taps=pltpu.VMEM((2, 6 * CH, 4 * CH), BF16),
        backward_taps=pltpu.VMEM((2, 6 * CH, 4 * CH), BF16),
        noise_taps=pltpu.VMEM((CH, NOISE), BF16),
        gains=pltpu.VMEM((5, CH, COLS), F32),
        edge_out=pltpu.VMEM((2, 8, COLS), F32),
        edge_in=pltpu.VMEM((2, 8, COLS), F32),
        target_tiles=pltpu.VMEM((3, 8, COLS), F32),
        weight_tiles=pltpu.VMEM((3, 8, COLS), F32),
        own_pred=pltpu.VMEM((3, HERE, 8, COLS), F32),
        all_pred=pltpu.VMEM((MEMS, 3, HERE, 8, COLS), F32),
        pred_grad=pltpu.VMEM((3, HERE, 8, COLS), F32),
        sums=pltpu.VMEM((5, CH, COLS), F32),
        tap_sum=pltpu.VMEM((2, 3 * CH, 256), F32),
        parts=pltpu.VMEM((2, 2, GROUP, 8, COLS), F32),
        core_in=pltpu.VMEM((2, GROUP, 8, COLS), F32),
        scattered=pltpu.VMEM((2, GROUP - 1, 8, COLS), F32),
        spread=pltpu.VMEM((2, DEPTH, 8, COLS), F32),
        small=pltpu.VMEM((8, 128), F32),
        small_core=pltpu.VMEM((8, 128), F32),
        small_in=pltpu.VMEM((GROUP, 8, 128), F32),
        small_line=pltpu.VMEM((DEPTH, 8, 128), F32),
        halo_sems=sems(2, 6),
        mem_sems=sems(3, 2, MEMS - 1),
        core_sems=sems(2, 5),
        plane_sems=sems(2, 2, GROUP - 1),
        line_sems=sems(2, 2, DEPTH - 1),
        back_sems=sems(2, 2, GROUP - 1),
        small_sems=sems(2, GROUP - 1),
        small_line_sems=sems(2, DEPTH - 1),
    )
    predictions, gathered, small = pl.pallas_call(
        step_kernel,
        out_shape=(
            jax.ShapeDtypeStruct((HERE, 2, ROWS, COLS), F32),
            jax.ShapeDtypeStruct((2, 2, GROUP, 8, COLS), F32),
            jax.ShapeDtypeStruct((8, 128), F32),
        ),
        in_specs=[far] * 9,
        out_specs=(vmem, vmem, vmem),
        scratch_shapes=list(scratch.values()),
        compiler_params=pltpu.CompilerParams(
            collective_id=0, has_side_effects=True, vmem_limit_bytes=VMEM_BYTES
        ),
        name="train_step",
    )(
        block_input,
        member_seeds,
        targets,
        land_mask,
        noise_weight.T,
        conv_weight,
        block_gain,
        head_weight,
        head_gain.reshape(1, CH),
    )
    loss, predictions, grad_conv, grad_block_gain, grad_head_weight, grad_head_gain, grad_noise = pl.pallas_call(
        unpack_kernel,
        out_shape=(
            jax.ShapeDtypeStruct((1, 1), F32),
            jax.ShapeDtypeStruct((HERE, 2, ROWS, COLS), F32),
            jax.ShapeDtypeStruct((2, 9, CH, CH), F32),
            jax.ShapeDtypeStruct((2, CH), F32),
            jax.ShapeDtypeStruct((2, CH), F32),
            jax.ShapeDtypeStruct((1, CH), F32),
            jax.ShapeDtypeStruct((NOISE, CH), F32),
        ),
        in_specs=[vmem] * 3,
        out_specs=(vmem,) * 7,
        scratch_shapes=[pltpu.VMEM((3 * CH, 256), F32)],
        compiler_params=pltpu.CompilerParams(vmem_limit_bytes=VMEM_BYTES),
        name="unpack",
    )(predictions, gathered, small)
    return (
        loss.reshape(()),
        predictions,
        grad_conv,
        grad_block_gain,
        grad_head_weight,
        grad_head_gain.reshape(CH),
        grad_noise.T,
    )


def solution(mesh):
    return jax.shard_map(
        on_device,
        mesh=mesh,
        in_specs=(
            P("mem", None, "tile", None),
            P("mem"),
            P(None, "tile", None),
            P("tile", None),
            P(),
            P(),
            P(),
            P(),
            P(),
        ),
        out_specs=(P(), P("mem", None, "tile", None), P(), P(), P(), P(), P()),
        check_vma=False,
    )
```

```python
import jax
import jax.numpy as jnp
from jax import lax
from jax.experimental import pallas as pl
from jax.experimental.pallas import tpu as pltpu
from jax.sharding import PartitionSpec as P

LOSS_SCALE = 16384
MESH_ID = pl.DeviceIdType.MESH
GROUP = 16
MEMS = 8
TILES = 32
HERE = 2
MEMBERS = 16
ROWS = 8
COLS = 256
CH = 64
NOISE = 8
HALO = 4
EXT = ROWS + 2 * HALO
GRID_ROWS = ROWS * TILES
PART = 6
DENSE = 9
DEPTH = 8
VMEM_BYTES = 63 * 2**20
F32 = jnp.float32
BF16 = jnp.bfloat16
eps_norm = 1e-05
smooth_sq = 0.01


def coordinates():
    mem, tile = lax.axis_index("mem"), lax.axis_index("tile")
    return mem // 2, (tile // 2) % 4, (tile // 8) * 2 + mem % 2, tile % 2


def device_at(x, y, z, core):
    return (x * 2 + z % 2, (z // 2) * 8 + y * 2 + core)


def plane_rank():
    x, y, _, _ = coordinates()
    return x * 4 + y


def plane_device(rank):
    _, _, z, core = coordinates()
    return device_at(rank // 4, rank % 4, z, core)


def depth_device(rank):
    x, y, _, core = coordinates()
    return device_at(x, y, rank, core)


def core_device(rank):
    x, y, z, _ = coordinates()
    return device_at(x, y, z, rank)


def mem_device(rank):
    return (rank, lax.axis_index("tile"))


def others(rank, count):
    return [lax.rem(rank + step, count) for step in range(1, count)]


def modulo(value, base):
    quotient = jnp.floor(value.astype(F32) * (1.0 / base)).astype(jnp.int32)
    rest = value - quotient * base
    rest = jnp.where(rest < 0, rest + base, rest)
    return jnp.where(rest >= base, rest - base, rest)


def noise_row(seed, row):
    channel = lax.broadcasted_iota(jnp.int32, (NOISE, COLS), 0)
    column = lax.broadcasted_iota(jnp.int32, (NOISE, COLS), 1)
    first = modulo(7919 * channel + column + (seed + row * COLS), 65521)
    second = modulo(first * 3001 + 12345, 65521)
    folded = modulo(second, 46337)
    third = modulo(folded * folded + second, 65521)
    fourth = modulo(third * 2897 + 4111, 65521)
    return ((fourth - 32760).astype(F32) / 18914.0).astype(BF16)


def columns_of(shape):
    return lax.broadcasted_iota(jnp.int32, shape, len(shape) - 1)


def from_left(value):
    return jnp.where(columns_of(value.shape) == 0, jnp.zeros((), value.dtype), pltpu.roll(value, 1, axis=1))


def from_right(value):
    return jnp.where(
        columns_of(value.shape) == COLS - 1, jnp.zeros((), value.dtype), pltpu.roll(value, COLS - 1, axis=1)
    )


def dot(left, right):
    return jnp.dot(left, right, preferred_element_type=F32)


def dot_rows(left, right):
    return lax.dot_general(left, right, (((1,), (1,)), ((), ())), preferred_element_type=F32)


def diagonal():
    shape = (CH, CH)
    return lax.broadcasted_iota(jnp.int32, shape, 0) == lax.broadcasted_iota(jnp.int32, shape, 1)


def as_column(row):
    return jnp.sum(jnp.where(diagonal(), jnp.broadcast_to(row, (CH, CH)), 0.0), axis=1, keepdims=True)


def as_row(column):
    return jnp.sum(jnp.where(diagonal(), jnp.broadcast_to(column, (CH, CH)), 0.0), axis=0, keepdims=True)


def silu_parts(value):
    gate = 0.5 * jnp.tanh(0.5 * value) + 0.5
    gated = value * gate
    return gated, gate + gated * (1.0 - gate)


def inverse_scale(stream):
    return lax.rsqrt(jnp.sum(stream * stream, axis=0, keepdims=True) * (1.0 / CH) + eps_norm)


def norm_back(grad, normed, inverse):
    mean = jnp.sum(grad * normed, axis=0, keepdims=True) * (1.0 / CH)
    return (grad - normed * mean) * inverse


def step_kernel(
    block_input_far,
    seeds_far,
    targets_far,
    land_mask_far,
    noise_weight_far,
    conv_weight_far,
    block_gain_far,
    head_weight_far,
    head_gain_far,
    predictions,
    gathered,
    small_out,
    block_input,
    seeds,
    targets,
    land_mask,
    noise_weight,
    conv_weight,
    block_gain,
    head_weight,
    head_gain,
    load_sems,
    turned,
    raw,
    noise,
    stream0,
    stream1,
    stream2,
    inverse0,
    inverse1,
    inverse2,
    slope0,
    slope1,
    inputs0,
    inputs1,
    grads0,
    grads1,
    stream_grad,
    head_in,
    forward_taps,
    backward_taps,
    noise_taps,
    gains,
    edge_out,
    edge_in,
    target_tiles,
    weight_tiles,
    own_pred,
    all_pred,
    pred_grad,
    sums,
    tap_sum,
    parts,
    core_in,
    scattered,
    spread,
    small,
    small_core,
    small_in,
    small_line,
    halo_sems,
    mem_sems,
    core_sems,
    plane_sems,
    line_sems,
    back_sems,
    small_sems,
    small_line_sems,
):
    mem, tile = lax.axis_index("mem"), lax.axis_index("tile")
    in_plane = plane_rank()
    _, _, depth, core = coordinates()
    other_core = 1 - core
    below, above = lax.rem(tile + 1, TILES), lax.rem(tile + TILES - 1, TILES)
    plane = [(plane_device(rank), rank) for rank in others(in_plane, GROUP)]
    line = [(depth_device(rank), rank) for rank in others(depth, DEPTH)]
    members = [(mem_device(rank), rank) for rank in others(mem, MEMS)]

    loads = [
        pltpu.make_async_copy(far, near, load_sems.at[at])
        for at, (far, near) in enumerate(
            (
                (block_input_far, block_input),
                (seeds_far, seeds),
                (targets_far, targets),
                (land_mask_far, land_mask),
                (noise_weight_far, noise_weight),
                (conv_weight_far, conv_weight),
                (block_gain_far, block_gain),
                (head_weight_far, head_weight),
                (head_gain_far, head_gain),
            )
        )
    ]
    for load in loads:
        load.start()

    barrier = pltpu.get_barrier_semaphore()
    for device in [(mem, below), (mem, above)] + [core_device(other_core)] + [
        d for d, _ in plane + line + members
    ]:
        pl.semaphore_signal(barrier, inc=1, device_id=device, device_id_type=MESH_ID)

    def send(source, target, sems, slot, device):
        copy = pltpu.make_async_remote_copy(
            src_ref=source,
            dst_ref=target,
            send_sem=sems.at[0, slot],
            recv_sem=sems.at[1, slot],
            device_id=device,
            device_id_type=MESH_ID,
        )
        copy.start()
        return copy

    def wait(copies):
        for copy in copies:
            copy.wait()

    loads[0].wait()
    for m in range(HERE):
        for half in range(2):
            lanes = pl.ds(128 * half, 128)
            turned[m, half] = block_input[m, :, :, lanes].astype(F32).reshape(CH * ROWS, 128)

    def bring(rows):
        for r in rows:
            for m in range(HERE):
                for half in range(2):
                    lanes = pl.ds(128 * half, 128)
                    raw[HALO + r, m, :, lanes] = turned[m, half, pl.ds(r, CH, stride=ROWS), :].astype(BF16)

    bring((0, 1, 6, 7))
    pl.semaphore_wait(barrier, 3 + (GROUP - 1) + (DEPTH - 1) + (MEMS - 1))

    def halo(up, down, up_to, down_to, slot):
        return [
            send(raw.at[pl.ds(up, 2)], raw.at[pl.ds(up_to, 2)], halo_sems, slot, (mem, above)),
            send(raw.at[pl.ds(down, 2)], raw.at[pl.ds(down_to, 2)], halo_sems, slot + 1, (mem, below)),
        ]

    near_copies = halo(4, 10, 12, 2, 0)
    bring(range(2, 6))
    far_copies = halo(6, 8, 14, 0, 2)
    wait(loads[1:])
    for side, start in ((0, 0), (1, ROWS - 2)):
        edge_out[side] = jnp.zeros((8, COLS), F32)
        for v in range(2):
            edge_out[side, pl.ds(2 * v, 2), :] = targets[v, pl.ds(start, 2), :]
        edge_out[side, pl.ds(4, 2), :] = land_mask[pl.ds(start, 2), :].astype(F32)
    far_copies += [
        send(edge_out.at[0], edge_in.at[1], halo_sems, 4, (mem, above)),
        send(edge_out.at[1], edge_in.at[0], halo_sems, 5, (mem, below)),
    ]

    unit = diagonal().astype(F32).astype(BF16)
    blank = jnp.zeros((CH, CH), BF16)
    for b in range(2):
        for dc in range(3):
            taps = [conv_weight[b, 3 * dr + dc] for dr in range(3)]
            turned_taps = [dot_rows(unit, tap).astype(BF16) for tap in taps]
            for ro in range(2):
                at = pl.ds((2 * dc + ro) * CH, CH)
                ahead = [blank] * ro + turned_taps + [blank] * (1 - ro)
                forward_taps[b, at, :] = dot_rows(unit, jnp.concatenate(ahead, axis=0)).astype(BF16)
                back = [blank] * ro + taps[::-1] + [blank] * (1 - ro)
                backward_taps[b, at, :] = dot_rows(unit, jnp.concatenate(back, axis=0)).astype(BF16)
    noise_taps[...] = dot_rows(unit, noise_weight[...]).astype(BF16)
    columns = [block_gain[pl.ds(0, 1), :], block_gain[pl.ds(1, 1), :], head_gain[...]]
    columns += [head_weight[pl.ds(v, 1), :].astype(F32) for v in range(2)]
    for at, row in enumerate(columns):
        gains[at] = jnp.broadcast_to(as_column(row), (CH, COLS))
    for at in range(5):
        sums[at] = jnp.zeros((CH, COLS), F32)
    tap_sum[...] = jnp.zeros_like(tap_sum)

    def inside(e):
        row = tile * ROWS - HALO + e
        return jnp.where((row >= 0) & (row < GRID_ROWS), 1.0, 0.0).astype(F32)

    def make_noise(e):
        row = jnp.clip(tile * ROWS - HALO + e, 0, GRID_ROWS - 1)
        for m in range(HERE):
            field = noise_row(seeds[m], row)
            noise[e, m] = field.astype(F32)
            stream0[e, m] = dot(noise_taps[...], field)

    def entry(e):
        for m in range(HERE):
            stream = raw[e, m].astype(F32) + stream0[e, m]
            stream0[e, m] = stream
            inverse = inverse_scale(stream)
            inverse0[e, m] = jnp.broadcast_to(inverse, (8, COLS))
            inputs0[e, m] = (stream * (inverse * inside(e)) * gains[0]).astype(BF16)

    def forward(b, e, ms=range(HERE)):
        source, stream_in, stream_out, slope = (
            (inputs0, stream0, stream1, slope0),
            (inputs1, stream1, stream2, slope1),
        )[b]
        for m in ms:
            window = source[pl.ds(e - 1, 4), m].reshape(4 * CH, COLS)
            taken = dot(forward_taps[b], window)
            for ro in range(2):
                left, middle, right = [taken[(2 * dc + ro) * CH : (2 * dc + ro + 1) * CH] for dc in range(3)]
                gated, bent = silu_parts(middle + from_left(left) + from_right(right))
                slope[e + ro, m] = bent
                stream = stream_in[e + ro, m] + gated
                stream_out[e + ro, m] = stream
                inverse = inverse_scale(stream)
                if b == 0:
                    inverse1[e + ro, m] = jnp.broadcast_to(inverse, (8, COLS))
                    inputs1[e + ro, m] = (stream * (inverse * inside(e + ro)) * gains[1]).astype(BF16)
                else:
                    inverse2[e + ro, m] = jnp.broadcast_to(inverse, (8, COLS))
                    headed = (stream * inverse * gains[2]).astype(BF16)
                    head_in[e + ro, m] = headed
                    found = dot(head_weight[...], headed)
                    place(own_pred, m, e + ro, found)

    def spots(e):
        if 6 <= e < 10:
            return [(0, e - 6), (0, e - 2)]
        part = 1 if HALO <= e < HALO + ROWS else 2
        at = e - HALO + 2 * part - 2 if e < 8 else e - HALO - ROWS + 6 - 2 * part
        return [(part, at), (part, at + 4)]

    def place(ref, m, e, pair):
        for v, (part, at) in enumerate(spots(e)):
            ref[part, m, pl.ds(at, 1), :] = pair[v : v + 1]

    def over(first, count, body):
        for i in range(count):
            body(first + 2 * i)

    def over_rows(first, count, body):
        for i in range(count):
            body(first + i)

    def share(part):
        all_pred[mem, part] = own_pred[part]
        return [
            send(own_pred.at[part], all_pred.at[mem, part], mem_sems.at[part], step, device)
            for step, (device, _) in enumerate(members)
        ]

    over_rows(HALO, ROWS, make_noise)
    over_rows(HALO, ROWS, entry)
    over(5, 3, lambda e: forward(0, e))
    over(6, 2, lambda e: forward(1, e))
    shared = [share(0)]
    over_rows(0, HALO, make_noise)
    over_rows(HALO + ROWS, HALO, make_noise)
    for v in range(2):
        target_tiles[0, pl.ds(4 * v, 4), :] = targets[v, pl.ds(2, 4), :]
        weight_tiles[0, pl.ds(4 * v, 4), :] = land_mask[pl.ds(2, 4), :].astype(F32)
        for side in range(2):
            at = pl.ds(4 * v + 2 * side, 2)
            target_tiles[1, at, :] = targets[v, pl.ds(6 * side, 2), :]
            weight_tiles[1, at, :] = land_mask[pl.ds(6 * side, 2), :].astype(F32)
    wait(near_copies)
    for e in (2, 3, 12, 13):
        entry(e)
    for b, e in ((0, 3), (0, 11), (1, 4), (1, 10)):
        forward(b, e)
    shared.append(share(1))
    wait(far_copies)
    for e in (0, 1, 14, 15):
        entry(e)
    for b, e in ((0, 1), (0, 13), (1, 2), (1, 12)):
        forward(b, e)
    shared.append(share(2))
    for v in range(2):
        for m in range(HERE):
            predictions[m, v, pl.ds(2, 4), :] = own_pred[0, m, pl.ds(4 * v, 4), :]
            for side in range(2):
                predictions[m, v, pl.ds(6 * side, 2), :] = own_pred[1, m, pl.ds(4 * v + 2 * side, 2), :]
        for side in range(2):
            at = pl.ds(4 * v + 2 * side, 2)
            target_tiles[2, at, :] = edge_in[side, pl.ds(2 * v, 2), :]
            weight_tiles[2, at, :] = edge_in[side, pl.ds(4, 2), :]
    place_in = lax.broadcasted_iota(jnp.int32, (8, COLS), 0) % 4
    for part, (first, second) in enumerate(((2, 4), (0, 6), (-2, 8))):
        rows = jnp.where(place_in < 2, place_in + first, place_in - 2 + second)
        area = 1.0 - 2.0 * (rows + tile * ROWS).astype(F32) / (3.0 * GRID_ROWS)
        weight_tiles[part] = area * (1.0 + weight_tiles[part])

    cells = GRID_ROWS * COLS

    def length_sq(gap):
        square = gap * gap
        return square + pltpu.roll(square, 4, axis=0) + smooth_sq

    def pull_apart(m, part):
        mine = own_pred[part, m]
        pull = jnp.zeros((8, COLS), F32)
        total = jnp.zeros((8, COLS), F32) - smooth_sq**0.5
        for n in range(MEMBERS):
            gap = mine - all_pred[n // HERE, part, n % HERE]
            square = length_sq(gap)
            inverse = lax.rsqrt(square)
            pull = pull + gap * inverse
            total = total + square * inverse
        miss = mine - target_tiles[part]
        square = length_sq(miss)
        inverse = lax.rsqrt(square)
        weights = weight_tiles[part]
        grad = (weights * (LOSS_SCALE / cells)) * (
            miss * inverse * (1.0 / MEMBERS) - pull * (1.0 / (MEMBERS * (MEMBERS - 1.0)))
        )
        pred_grad[part, m] = grad.astype(BF16).astype(F32)
        return weights * (
            square * inverse * (1.0 / MEMBERS) - total * (1.0 / (2.0 * MEMBERS * (MEMBERS - 1)))
        )

    def top(e, own):
        for m in range(HERE):
            (part0, at0), (part1, at1) = spots(e)
            pull0 = pred_grad[part0, m, pl.ds(at0, 1), :]
            pull1 = pred_grad[part1, m, pl.ds(at1, 1), :]
            grad = gains[3] * pull0 + gains[4] * pull1
            inverse = inverse2[e, m, pl.ds(0, 1), :]
            normed = stream2[e, m] * inverse
            if own:
                headed = head_in[e, m].astype(F32)
                sums[2] += grad * normed
                sums[3] += headed * pull0
                sums[4] += headed * pull1
            grad = norm_back(grad * gains[2], normed, inverse)
            stream_grad[e, m] = grad
            grads1[e, m] = (grad * (slope1[e, m] * inside(e))).astype(BF16)

    def tap_grads(b, rows, fresh):
        grads, inputs = ((grads0, inputs0), (grads1, inputs1))[b]
        shifted, windows = [], []
        for e in rows:
            for m in range(HERE):
                grad = grads[e, m]
                shifted.append(jnp.concatenate([from_right(grad), grad, from_left(grad)], axis=0))
                windows.append(inputs[pl.ds(e - 1, 3), m].reshape(3 * CH, COLS))
        found = dot_rows(jnp.concatenate(shifted, axis=1), jnp.concatenate(windows, axis=1))
        at = pl.ds(0, 3 * CH)
        tap_sum[b, :, at] = found if fresh else tap_sum[b, :, at] + found

    def backward(b, e, last):
        source, stream, inverses = ((grads0, stream0, inverse0), (grads1, stream1, inverse1))[b]
        for m in range(HERE):
            window = source[pl.ds(e - 1, 4), m].reshape(4 * CH, COLS)
            taken = dot(backward_taps[b], window)
            for ro in range(2):
                left, middle, right = [taken[(2 * dc + ro) * CH : (2 * dc + ro + 1) * CH] for dc in range(3)]
                grad = middle + from_right(left) + from_left(right)
                inverse = inverses[e + ro, m, pl.ds(0, 1), :]
                normed = stream[e + ro, m] * inverse
                counted = HALO <= e + ro < HALO + ROWS
                if counted:
                    sums[b] += grad * normed
                total = stream_grad[e + ro, m] + norm_back(grad * gains[b], normed, inverse)
                if b == 1:
                    stream_grad[e + ro, m] = total
                    grads0[e + ro, m] = (total * (slope0[e + ro, m] * inside(e + ro))).astype(BF16)
                else:
                    last(e + ro, m, total.astype(BF16))

    def across(source, target, sems, slot):
        return [send(source, target, sems, slot, core_device(other_core))]

    def to_core(b):
        for half in range(2):
            for at in range(GROUP):
                first = PART * (GROUP * half + at)
                parts[b, half, at, pl.ds(0, PART), :] = tap_sum[b, pl.ds(first, PART), pl.ds(0, 128)]
                for side in range(2):
                    rest = tap_sum[b, pl.ds(first + 3 * side, 3), pl.ds(128, CH)]
                    parts[b, half, at, pl.ds(PART, 3), pl.ds(CH * side, CH)] = rest
        return across(parts.at[b, other_core], core_in.at[b], core_sems, b)

    def to_plane(b):
        parts[b, core] = parts[b, core] + core_in[b]
        return [
            send(parts.at[b, core, rank], scattered.at[b, step], plane_sems.at[b], step, device)
            for step, (device, rank) in enumerate(plane)
        ]

    def to_depth(b):
        total = parts[b, core, in_plane]
        for step in range(GROUP - 1):
            total = total + scattered[b, step]
        spread[b, depth] = total
        return [
            send(spread.at[b, depth], spread.at[b, depth], line_sems.at[b], step, device)
            for step, (device, _) in enumerate(line)
        ]

    def to_plane_again(b):
        total = spread[b, 0]
        for rank in range(1, DEPTH):
            total = total + spread[b, rank]
        gathered[b, core, in_plane] = total
        mine = gathered.at[b, core, in_plane]
        return [send(mine, mine, back_sems.at[b], step, device) for step, (device, _) in enumerate(plane)]

    def to_core_again(b):
        return across(gathered.at[b, core], gathered.at[b, core], core_sems, 2 + b)

    def grads_of(part):
        found = jnp.zeros((8, COLS), F32)
        for m in range(HERE):
            found += pull_apart(m, part)
        return found

    wait(shared[0])
    loss_tile = grads_of(0)
    over_rows(6, 4, lambda e: top(e, True))
    tap_grads(1, range(6, 10), True)
    backward(1, 7, None)
    wait(shared[1])
    loss_tile += grads_of(1)
    for e in (4, 5, 10, 11):
        top(e, True)
    tap_grads(1, (4, 5, 10, 11), False)
    core_1 = to_core(1)
    backward(1, 5, None)
    backward(1, 9, None)
    wait(core_1)
    plane_1 = to_plane(1)
    tap_grads(0, range(5, 11), True)
    wait(shared[2])
    grads_of(2)
    for e in (2, 3, 12, 13):
        top(e, False)
    for e in (3, 11):
        backward(1, e, None)
    tap_grads(0, (4, 11), False)
    core_0 = to_core(0)

    small[...] = jnp.zeros_like(small)
    sum_noise = tap_sum.at[0, pl.ds(0, CH), pl.ds(0, NOISE)]
    sum_noise[...] = jnp.zeros((CH, NOISE), F32)

    def last(e, m, entry_grad):
        sum_noise[...] += dot_rows(entry_grad, noise[e, m].astype(BF16))

    over(4, 2, lambda e: backward(0, e, last))
    wait(core_0)
    plane_0 = to_plane(0)
    over(8, 2, lambda e: backward(0, e, last))
    column = lax.broadcasted_iota(jnp.int32, (CH, NOISE), 1)
    late = sum_noise[...]
    rows = [as_row(jnp.sum(sums[at], axis=1, keepdims=True)) for at in range(5)]
    for k in range(NOISE):
        rows.append(as_row(jnp.sum(jnp.where(column == k, late, 0.0), axis=1, keepdims=True)))
    loss = jnp.sum(jnp.sum(loss_tile, axis=0, keepdims=True), axis=1, keepdims=True) * (0.5 / cells)
    rows.append(jnp.broadcast_to(loss, (1, CH)))
    for at, row in enumerate(rows):
        small[pl.ds(at // 2, 1), pl.ds(CH * (at % 2), CH)] = row
    small_0 = across(small, small_core, core_sems, 4)
    wait(plane_1)
    depth_1 = to_depth(1)
    wait(small_0)
    small_in[in_plane] = small[...] + small_core[...]
    mine = small_in.at[in_plane]
    small_1 = [send(mine, mine, small_sems, step, device) for step, (device, _) in enumerate(plane)]
    wait(plane_0)
    depth_0 = to_depth(0)
    wait(depth_1)
    back_1 = to_plane_again(1)
    wait(small_1)
    total = small_in[0]
    for rank in range(1, GROUP):
        total = total + small_in[rank]
    small_line[depth] = total
    mine = small_line.at[depth]
    small_2 = [send(mine, mine, small_line_sems, step, device) for step, (device, _) in enumerate(line)]
    wait(depth_0)
    back_0 = to_plane_again(0)
    wait(back_1)
    last_1 = to_core_again(1)
    wait(small_2)
    total = small_line[0]
    for rank in range(1, DEPTH):
        total = total + small_line[rank]
    small_out[...] = total
    wait(back_0)
    last_0 = to_core_again(0)
    wait(last_1 + last_0)


def unpack_kernel(
    predictions, gathered, small, loss, pred_out, grad_conv, grad_gain, grad_head, grad_head_gain, grad_noise, whole
):
    pred_out[...] = predictions[...]
    for b in range(2):
        for half in range(2):
            for at in range(GROUP):
                first = PART * (GROUP * half + at)
                whole[pl.ds(first, PART), pl.ds(0, 128)] = gathered[b, half, at, pl.ds(0, PART), :]
                for side in range(2):
                    rest = gathered[b, half, at, pl.ds(PART, 3), pl.ds(CH * side, CH)]
                    whole[pl.ds(first + 3 * side, 3), pl.ds(128, CH)] = rest
        for dr in range(3):
            for dc in range(3):
                grad_conv[b, 3 * dr + dc] = whole[pl.ds(CH * dc, CH), pl.ds(CH * dr, CH)]
    for out, first, count in ((grad_gain, 0, 2), (grad_head_gain, 2, 1), (grad_head, 3, 2), (grad_noise, 5, NOISE)):
        for at in range(count):
            out[pl.ds(at, 1), :] = small[pl.ds((first + at) // 2, 1), pl.ds(CH * ((first + at) % 2), CH)]
    loss[...] = small[pl.ds(6, 1), pl.ds(CH, 1)]


def on_device(
    block_input,
    member_seeds,
    targets,
    land_mask,
    noise_weight,
    conv_weight,
    block_gain,
    head_weight,
    head_gain,
):
    vmem = pl.BlockSpec(memory_space=pltpu.VMEM)
    far = pl.BlockSpec(memory_space=pltpu.HBM)

    def field(*shape):
        return pltpu.VMEM((EXT, HERE) + shape, F32)

    def half(*shape):
        return pltpu.VMEM((EXT, HERE) + shape, BF16)

    def sems(*shape):
        return pltpu.SemaphoreType.DMA(shape)

    scratch = dict(
        block_input=pltpu.VMEM(block_input.shape, BF16),
        seeds=pltpu.SMEM(member_seeds.shape, jnp.int32),
        targets=pltpu.VMEM(targets.shape, F32),
        land_mask=pltpu.VMEM(land_mask.shape, jnp.int32),
        noise_weight=pltpu.VMEM((NOISE, CH), BF16),
        conv_weight=pltpu.VMEM(conv_weight.shape, BF16),
        block_gain=pltpu.VMEM(block_gain.shape, F32),
        head_weight=pltpu.VMEM(head_weight.shape, BF16),
        head_gain=pltpu.VMEM((1, CH), F32),
        load_sems=sems(9),
        turned=pltpu.VMEM((HERE, 2, CH * ROWS, 128), F32),
        raw=half(CH, COLS),
        noise=field(NOISE, COLS),
        stream0=field(CH, COLS),
        stream1=field(CH, COLS),
        stream2=field(CH, COLS),
        inverse0=field(8, COLS),
        inverse1=field(8, COLS),
        inverse2=field(8, COLS),
        slope0=field(CH, COLS),
        slope1=field(CH, COLS),
        inputs0=half(CH, COLS),
        inputs1=half(CH, COLS),
        grads0=half(CH, COLS),
        grads1=half(CH, COLS),
        stream_grad=field(CH, COLS),
        head_in=half(CH, COLS),
        forward_taps=pltpu.VMEM((2, 6 * CH, 4 * CH), BF16),
        backward_taps=pltpu.VMEM((2, 6 * CH, 4 * CH), BF16),
        noise_taps=pltpu.VMEM((CH, NOISE), BF16),
        gains=pltpu.VMEM((5, CH, COLS), F32),
        edge_out=pltpu.VMEM((2, 8, COLS), F32),
        edge_in=pltpu.VMEM((2, 8, COLS), F32),
        target_tiles=pltpu.VMEM((3, 8, COLS), F32),
        weight_tiles=pltpu.VMEM((3, 8, COLS), F32),
        own_pred=pltpu.VMEM((3, HERE, 8, COLS), F32),
        all_pred=pltpu.VMEM((MEMS, 3, HERE, 8, COLS), F32),
        pred_grad=pltpu.VMEM((3, HERE, 8, COLS), F32),
        sums=pltpu.VMEM((5, CH, COLS), F32),
        tap_sum=pltpu.VMEM((2, 3 * CH, 256), F32),
        parts=pltpu.VMEM((2, 2, GROUP, DENSE, 128), F32),
        core_in=pltpu.VMEM((2, GROUP, DENSE, 128), F32),
        scattered=pltpu.VMEM((2, GROUP - 1, DENSE, 128), F32),
        spread=pltpu.VMEM((2, DEPTH, DENSE, 128), F32),
        small=pltpu.VMEM((8, 128), F32),
        small_core=pltpu.VMEM((8, 128), F32),
        small_in=pltpu.VMEM((GROUP, 8, 128), F32),
        small_line=pltpu.VMEM((DEPTH, 8, 128), F32),
        halo_sems=sems(2, 6),
        mem_sems=sems(3, 2, MEMS - 1),
        core_sems=sems(2, 5),
        plane_sems=sems(2, 2, GROUP - 1),
        line_sems=sems(2, 2, DEPTH - 1),
        back_sems=sems(2, 2, GROUP - 1),
        small_sems=sems(2, GROUP - 1),
        small_line_sems=sems(2, DEPTH - 1),
    )
    predictions, gathered, small = pl.pallas_call(
        step_kernel,
        out_shape=(
            jax.ShapeDtypeStruct((HERE, 2, ROWS, COLS), F32),
            jax.ShapeDtypeStruct((2, 2, GROUP, DENSE, 128), F32),
            jax.ShapeDtypeStruct((8, 128), F32),
        ),
        in_specs=[far] * 9,
        out_specs=(vmem, vmem, vmem),
        scratch_shapes=list(scratch.values()),
        compiler_params=pltpu.CompilerParams(
            collective_id=0, has_side_effects=True, vmem_limit_bytes=VMEM_BYTES
        ),
        name="train_step",
    )(
        block_input,
        member_seeds,
        targets,
        land_mask,
        noise_weight.T,
        conv_weight,
        block_gain,
        head_weight,
        head_gain.reshape(1, CH),
    )
    loss, predictions, grad_conv, grad_block_gain, grad_head_weight, grad_head_gain, grad_noise = pl.pallas_call(
        unpack_kernel,
        out_shape=(
            jax.ShapeDtypeStruct((1, 1), F32),
            jax.ShapeDtypeStruct((HERE, 2, ROWS, COLS), F32),
            jax.ShapeDtypeStruct((2, 9, CH, CH), F32),
            jax.ShapeDtypeStruct((2, CH), F32),
            jax.ShapeDtypeStruct((2, CH), F32),
            jax.ShapeDtypeStruct((1, CH), F32),
            jax.ShapeDtypeStruct((NOISE, CH), F32),
        ),
        in_specs=[vmem] * 3,
        out_specs=(vmem,) * 7,
        scratch_shapes=[pltpu.VMEM((3 * CH, 256), F32)],
        compiler_params=pltpu.CompilerParams(vmem_limit_bytes=VMEM_BYTES),
        name="unpack",
    )(predictions, gathered, small)
    return (
        loss.reshape(()),
        predictions,
        grad_conv,
        grad_block_gain,
        grad_head_weight,
        grad_head_gain.reshape(CH),
        grad_noise.T,
    )


def solution(mesh):
    return jax.shard_map(
        on_device,
        mesh=mesh,
        in_specs=(
            P("mem", None, "tile", None),
            P("mem"),
            P(None, "tile", None),
            P("tile", None),
            P(),
            P(),
            P(),
            P(),
            P(),
        ),
        out_specs=(P(), P("mem", None, "tile", None), P(), P(), P(), P(), P()),
        check_vma=False,
    )
```

```python
import jax
import jax.numpy as jnp
from jax import lax
from jax.experimental import pallas as pl
from jax.experimental.pallas import tpu as pltpu
from jax.sharding import PartitionSpec as P

LOSS_SCALE = 16384
MESH_ID = pl.DeviceIdType.MESH
GROUP = 16
MEMS = 8
TILES = 32
HERE = 2
MEMBERS = 16
ROWS = 8
COLS = 256
CH = 64
NOISE = 8
HALO = 4
EXT = ROWS + 2 * HALO
GRID_ROWS = ROWS * TILES
PART = 6
DENSE = 9
DEPTH = 8
VMEM_BYTES = 63 * 2**20
F32 = jnp.float32
BF16 = jnp.bfloat16
eps_norm = 1e-05
smooth_sq = 0.01


def coordinates():
    mem, tile = lax.axis_index("mem"), lax.axis_index("tile")
    return mem // 2, (tile // 2) % 4, (tile // 8) * 2 + mem % 2, tile % 2


def device_at(x, y, z, core):
    return (x * 2 + z % 2, (z // 2) * 8 + y * 2 + core)


def plane_rank():
    x, y, _, _ = coordinates()
    return x * 4 + y


def plane_device(rank):
    _, _, z, core = coordinates()
    return device_at(rank // 4, rank % 4, z, core)


def depth_device(rank):
    x, y, _, core = coordinates()
    return device_at(x, y, rank, core)


def core_device(rank):
    x, y, z, _ = coordinates()
    return device_at(x, y, z, rank)


def mem_device(rank):
    return (rank, lax.axis_index("tile"))


def others(rank, count):
    return [lax.rem(rank + step, count) for step in range(1, count)]


def modulo(value, base):
    quotient = jnp.floor(value.astype(F32) * (1.0 / base)).astype(jnp.int32)
    rest = value - quotient * base
    rest = jnp.where(rest < 0, rest + base, rest)
    return jnp.where(rest >= base, rest - base, rest)


def noise_row(seed, row):
    channel = lax.broadcasted_iota(jnp.int32, (NOISE, COLS), 0)
    column = lax.broadcasted_iota(jnp.int32, (NOISE, COLS), 1)
    first = modulo(7919 * channel + column + (seed + row * COLS), 65521)
    second = modulo(first * 3001 + 12345, 65521)
    folded = modulo(second, 46337)
    third = modulo(folded * folded + second, 65521)
    fourth = modulo(third * 2897 + 4111, 65521)
    return ((fourth - 32760).astype(F32) / 18914.0).astype(BF16)


def columns_of(shape):
    return lax.broadcasted_iota(jnp.int32, shape, len(shape) - 1)


def from_left(value):
    return jnp.where(columns_of(value.shape) == 0, jnp.zeros((), value.dtype), pltpu.roll(value, 1, axis=1))


def from_right(value):
    return jnp.where(
        columns_of(value.shape) == COLS - 1, jnp.zeros((), value.dtype), pltpu.roll(value, COLS - 1, axis=1)
    )


def dot(left, right):
    return jnp.dot(left, right, preferred_element_type=F32)


def dot_rows(left, right):
    return lax.dot_general(left, right, (((1,), (1,)), ((), ())), preferred_element_type=F32)


def diagonal():
    shape = (CH, CH)
    return lax.broadcasted_iota(jnp.int32, shape, 0) == lax.broadcasted_iota(jnp.int32, shape, 1)


def as_column(row):
    return jnp.sum(jnp.where(diagonal(), jnp.broadcast_to(row, (CH, CH)), 0.0), axis=1, keepdims=True)


def as_row(column):
    return jnp.sum(jnp.where(diagonal(), jnp.broadcast_to(column, (CH, CH)), 0.0), axis=0, keepdims=True)


def silu_parts(value):
    gate = 0.5 * jnp.tanh(0.5 * value) + 0.5
    gated = value * gate
    return gated, gate + gated * (1.0 - gate)


def inverse_scale(stream):
    return lax.rsqrt(jnp.sum(stream * stream, axis=0, keepdims=True) * (1.0 / CH) + eps_norm)


def norm_back(grad, normed, inverse):
    mean = jnp.sum(grad * normed, axis=0, keepdims=True) * (1.0 / CH)
    return (grad - normed * mean) * inverse


def step_kernel(
    block_input_far,
    seeds_far,
    targets_far,
    land_mask_far,
    noise_weight_far,
    conv_weight_far,
    block_gain_far,
    head_weight_far,
    head_gain_far,
    predictions,
    gathered,
    small_out,
    block_input,
    seeds,
    targets,
    land_mask,
    noise_weight,
    conv_weight,
    block_gain,
    head_weight,
    head_gain,
    load_sems,
    turned,
    raw,
    noise,
    stream0,
    stream1,
    stream2,
    inverse0,
    inverse1,
    inverse2,
    slope0,
    slope1,
    inputs0,
    inputs1,
    grads0,
    grads1,
    stream_grad,
    head_in,
    forward_taps,
    backward_taps,
    noise_taps,
    gains,
    edge_out,
    edge_in,
    target_tiles,
    weight_tiles,
    own_pred,
    all_pred,
    pred_grad,
    sums,
    tap_sum,
    parts,
    core_in,
    scattered,
    spread,
    small,
    small_core,
    small_in,
    small_line,
    halo_sems,
    mem_sems,
    core_sems,
    plane_sems,
    line_sems,
    back_sems,
    small_sems,
    small_line_sems,
):
    mem, tile = lax.axis_index("mem"), lax.axis_index("tile")
    in_plane = plane_rank()
    _, _, depth, core = coordinates()
    other_core = 1 - core
    below, above = lax.rem(tile + 1, TILES), lax.rem(tile + TILES - 1, TILES)
    plane = [(plane_device(rank), rank) for rank in others(in_plane, GROUP)]
    line = [(depth_device(rank), rank) for rank in others(depth, DEPTH)]
    members = [(mem_device(rank), rank) for rank in others(mem, MEMS)]

    loads = [
        pltpu.make_async_copy(far, near, load_sems.at[at])
        for at, (far, near) in enumerate(
            (
                (block_input_far, block_input),
                (seeds_far, seeds),
                (targets_far, targets),
                (land_mask_far, land_mask),
                (noise_weight_far, noise_weight),
                (conv_weight_far, conv_weight),
                (block_gain_far, block_gain),
                (head_weight_far, head_weight),
                (head_gain_far, head_gain),
            )
        )
    ]
    for load in loads:
        load.start()

    barrier = pltpu.get_barrier_semaphore()
    for device in [(mem, below), (mem, above)] + [core_device(other_core)] + [
        d for d, _ in plane + line + members
    ]:
        pl.semaphore_signal(barrier, inc=1, device_id=device, device_id_type=MESH_ID)

    def send(source, target, sems, slot, device):
        copy = pltpu.make_async_remote_copy(
            src_ref=source,
            dst_ref=target,
            send_sem=sems.at[0, slot],
            recv_sem=sems.at[1, slot],
            device_id=device,
            device_id_type=MESH_ID,
        )
        copy.start()
        return copy

    def wait(copies):
        for copy in copies:
            copy.wait()

    loads[0].wait()
    for m in range(HERE):
        for half in range(2):
            lanes = pl.ds(128 * half, 128)
            turned[m, half] = block_input[m, :, :, lanes].astype(F32).reshape(CH * ROWS, 128)

    def bring(rows):
        for r in rows:
            for m in range(HERE):
                for half in range(2):
                    lanes = pl.ds(128 * half, 128)
                    raw[HALO + r, m, :, lanes] = turned[m, half, pl.ds(r, CH, stride=ROWS), :].astype(BF16)

    bring((0, 1, 6, 7))
    pl.semaphore_wait(barrier, 3 + (GROUP - 1) + (DEPTH - 1) + (MEMS - 1))

    def halo(up, down, up_to, down_to, slot):
        return [
            send(raw.at[pl.ds(up, 2)], raw.at[pl.ds(up_to, 2)], halo_sems, slot, (mem, above)),
            send(raw.at[pl.ds(down, 2)], raw.at[pl.ds(down_to, 2)], halo_sems, slot + 1, (mem, below)),
        ]

    near_copies = halo(4, 10, 12, 2, 0)
    bring(range(2, 6))
    far_copies = halo(6, 8, 14, 0, 2)
    wait(loads[1:])
    for side, start in ((0, 0), (1, ROWS - 2)):
        edge_out[side] = jnp.zeros((8, COLS), F32)
        for v in range(2):
            edge_out[side, pl.ds(2 * v, 2), :] = targets[v, pl.ds(start, 2), :]
        edge_out[side, pl.ds(4, 2), :] = land_mask[pl.ds(start, 2), :].astype(F32)
    far_copies += [
        send(edge_out.at[0], edge_in.at[1], halo_sems, 4, (mem, above)),
        send(edge_out.at[1], edge_in.at[0], halo_sems, 5, (mem, below)),
    ]

    unit = diagonal().astype(F32).astype(BF16)
    blank = jnp.zeros((CH, CH), BF16)
    for b in range(2):
        for dc in range(3):
            taps = [conv_weight[b, 3 * dr + dc] for dr in range(3)]
            turned_taps = [dot_rows(unit, tap).astype(BF16) for tap in taps]
            for ro in range(2):
                at = pl.ds((2 * dc + ro) * CH, CH)
                ahead = [blank] * ro + turned_taps + [blank] * (1 - ro)
                forward_taps[b, at, :] = dot_rows(unit, jnp.concatenate(ahead, axis=0)).astype(BF16)
                back = [blank] * ro + taps[::-1] + [blank] * (1 - ro)
                backward_taps[b, at, :] = dot_rows(unit, jnp.concatenate(back, axis=0)).astype(BF16)
    noise_taps[...] = dot_rows(unit, noise_weight[...]).astype(BF16)
    columns = [block_gain[pl.ds(0, 1), :], block_gain[pl.ds(1, 1), :], head_gain[...]]
    columns += [head_weight[pl.ds(v, 1), :].astype(F32) for v in range(2)]
    for at, row in enumerate(columns):
        gains[at] = jnp.broadcast_to(as_column(row), (CH, COLS))
    for at in range(5):
        sums[at] = jnp.zeros((CH, COLS), F32)
    tap_sum[...] = jnp.zeros_like(tap_sum)

    def inside(e):
        row = tile * ROWS - HALO + e
        return jnp.where((row >= 0) & (row < GRID_ROWS), 1.0, 0.0).astype(F32)

    def make_noise(e):
        row = jnp.clip(tile * ROWS - HALO + e, 0, GRID_ROWS - 1)
        for m in range(HERE):
            field = noise_row(seeds[m], row)
            noise[e, m] = field.astype(F32)
            stream0[e, m] = dot(noise_taps[...], field)

    def entry(e):
        for m in range(HERE):
            stream = raw[e, m].astype(F32) + stream0[e, m]
            stream0[e, m] = stream
            inverse = inverse_scale(stream)
            inverse0[e, m] = jnp.broadcast_to(inverse, (8, COLS))
            inputs0[e, m] = (stream * (inverse * inside(e)) * gains[0]).astype(BF16)

    def forward(b, e, ms=range(HERE)):
        source, stream_in, stream_out, slope = (
            (inputs0, stream0, stream1, slope0),
            (inputs1, stream1, stream2, slope1),
        )[b]
        for m in ms:
            window = source[pl.ds(e - 1, 4), m].reshape(4 * CH, COLS)
            taken = dot(forward_taps[b], window)
            for ro in range(2):
                left, middle, right = [taken[(2 * dc + ro) * CH : (2 * dc + ro + 1) * CH] for dc in range(3)]
                gated, bent = silu_parts(middle + from_left(left) + from_right(right))
                slope[e + ro, m] = bent
                stream = stream_in[e + ro, m] + gated
                stream_out[e + ro, m] = stream
                inverse = inverse_scale(stream)
                if b == 0:
                    inverse1[e + ro, m] = jnp.broadcast_to(inverse, (8, COLS))
                    inputs1[e + ro, m] = (stream * (inverse * inside(e + ro)) * gains[1]).astype(BF16)
                else:
                    inverse2[e + ro, m] = jnp.broadcast_to(inverse, (8, COLS))
                    headed = (stream * inverse * gains[2]).astype(BF16)
                    head_in[e + ro, m] = headed
                    found = dot(head_weight[...], headed)
                    place(own_pred, m, e + ro, found)

    def spots(e):
        if 6 <= e < 10:
            return [(0, e - 6), (0, e - 2)]
        part = 1 if HALO <= e < HALO + ROWS else 2
        at = e - HALO + 2 * part - 2 if e < 8 else e - HALO - ROWS + 6 - 2 * part
        return [(part, at), (part, at + 4)]

    def place(ref, m, e, pair):
        for v, (part, at) in enumerate(spots(e)):
            ref[part, m, pl.ds(at, 1), :] = pair[v : v + 1]

    def over(first, count, body):
        for i in range(count):
            body(first + 2 * i)

    def over_rows(first, count, body):
        for i in range(count):
            body(first + i)

    def share(part):
        all_pred[mem, part] = own_pred[part]
        return [
            send(own_pred.at[part], all_pred.at[mem, part], mem_sems.at[part], step, device)
            for step, (device, _) in enumerate(members)
        ]

    over_rows(HALO, ROWS, make_noise)
    over_rows(HALO, ROWS, entry)
    over(5, 3, lambda e: forward(0, e))
    over(6, 2, lambda e: forward(1, e))
    shared = [share(0)]
    over_rows(0, HALO, make_noise)
    over_rows(HALO + ROWS, HALO, make_noise)
    for v in range(2):
        target_tiles[0, pl.ds(4 * v, 4), :] = targets[v, pl.ds(2, 4), :]
        weight_tiles[0, pl.ds(4 * v, 4), :] = land_mask[pl.ds(2, 4), :].astype(F32)
        for side in range(2):
            at = pl.ds(4 * v + 2 * side, 2)
            target_tiles[1, at, :] = targets[v, pl.ds(6 * side, 2), :]
            weight_tiles[1, at, :] = land_mask[pl.ds(6 * side, 2), :].astype(F32)
    wait(near_copies)
    for e in (2, 3, 12, 13):
        entry(e)
    for b, e in ((0, 3), (0, 11), (1, 4), (1, 10)):
        forward(b, e)
    shared.append(share(1))
    wait(far_copies)
    for e in (0, 1, 14, 15):
        entry(e)
    for b, e in ((0, 1), (0, 13), (1, 2), (1, 12)):
        forward(b, e)
    shared.append(share(2))
    for v in range(2):
        for m in range(HERE):
            predictions[m, v, pl.ds(2, 4), :] = own_pred[0, m, pl.ds(4 * v, 4), :]
            for side in range(2):
                predictions[m, v, pl.ds(6 * side, 2), :] = own_pred[1, m, pl.ds(4 * v + 2 * side, 2), :]
        for side in range(2):
            at = pl.ds(4 * v + 2 * side, 2)
            target_tiles[2, at, :] = edge_in[side, pl.ds(2 * v, 2), :]
            weight_tiles[2, at, :] = edge_in[side, pl.ds(4, 2), :]
    place_in = lax.broadcasted_iota(jnp.int32, (8, COLS), 0) % 4
    for part, (first, second) in enumerate(((2, 4), (0, 6), (-2, 8))):
        rows = jnp.where(place_in < 2, place_in + first, place_in - 2 + second)
        area = 1.0 - 2.0 * (rows + tile * ROWS).astype(F32) / (3.0 * GRID_ROWS)
        weight_tiles[part] = area * (1.0 + weight_tiles[part])

    cells = GRID_ROWS * COLS

    def length_sq(gap):
        square = gap * gap
        return square + pltpu.roll(square, 4, axis=0) + smooth_sq

    def pull_apart(m, part):
        mine = own_pred[part, m]
        pull = jnp.zeros((8, COLS), F32)
        total = jnp.zeros((8, COLS), F32) - smooth_sq**0.5
        for n in range(MEMBERS):
            gap = mine - all_pred[n // HERE, part, n % HERE]
            square = length_sq(gap)
            inverse = lax.rsqrt(square)
            pull = pull + gap * inverse
            total = total + square * inverse
        miss = mine - target_tiles[part]
        square = length_sq(miss)
        inverse = lax.rsqrt(square)
        weights = weight_tiles[part]
        grad = (weights * (LOSS_SCALE / cells)) * (
            miss * inverse * (1.0 / MEMBERS) - pull * (1.0 / (MEMBERS * (MEMBERS - 1.0)))
        )
        pred_grad[part, m] = grad.astype(BF16).astype(F32)
        return weights * (
            square * inverse * (1.0 / MEMBERS) - total * (1.0 / (2.0 * MEMBERS * (MEMBERS - 1)))
        )

    def top(e, own):
        for m in range(HERE):
            (part0, at0), (part1, at1) = spots(e)
            pull0 = pred_grad[part0, m, pl.ds(at0, 1), :]
            pull1 = pred_grad[part1, m, pl.ds(at1, 1), :]
            grad = gains[3] * pull0 + gains[4] * pull1
            inverse = inverse2[e, m, pl.ds(0, 1), :]
            normed = stream2[e, m] * inverse
            if own:
                headed = head_in[e, m].astype(F32)
                sums[2] += grad * normed
                sums[3] += headed * pull0
                sums[4] += headed * pull1
            grad = norm_back(grad * gains[2], normed, inverse)
            stream_grad[e, m] = grad
            grads1[e, m] = (grad * (slope1[e, m] * inside(e))).astype(BF16)

    def tap_grads(b, rows, fresh):
        grads, inputs = ((grads0, inputs0), (grads1, inputs1))[b]
        shifted, windows = [], []
        for e in rows:
            for m in range(HERE):
                grad = grads[e, m]
                shifted.append(jnp.concatenate([from_right(grad), grad, from_left(grad)], axis=0))
                windows.append(inputs[pl.ds(e - 1, 3), m].reshape(3 * CH, COLS))
        found = dot_rows(jnp.concatenate(shifted, axis=1), jnp.concatenate(windows, axis=1))
        at = pl.ds(0, 3 * CH)
        rows_here = pl.ds(0, 3 * CH)
        tap_sum[b, rows_here, at] = found if fresh else tap_sum[b, rows_here, at] + found

    def backward(b, e, last):
        source, stream, inverses = ((grads0, stream0, inverse0), (grads1, stream1, inverse1))[b]
        for m in range(HERE):
            window = source[pl.ds(e - 1, 4), m].reshape(4 * CH, COLS)
            taken = dot(backward_taps[b], window)
            for ro in range(2):
                left, middle, right = [taken[(2 * dc + ro) * CH : (2 * dc + ro + 1) * CH] for dc in range(3)]
                grad = middle + from_right(left) + from_left(right)
                inverse = inverses[e + ro, m, pl.ds(0, 1), :]
                normed = stream[e + ro, m] * inverse
                counted = HALO <= e + ro < HALO + ROWS
                if counted:
                    sums[b] += grad * normed
                total = stream_grad[e + ro, m] + norm_back(grad * gains[b], normed, inverse)
                if b == 1:
                    stream_grad[e + ro, m] = total
                    grads0[e + ro, m] = (total * (slope0[e + ro, m] * inside(e + ro))).astype(BF16)
                else:
                    last(e + ro, m, total.astype(BF16))

    def across(source, target, sems, slot):
        return [send(source, target, sems, slot, core_device(other_core))]

    def to_core(b):
        for half in range(2):
            for at in range(GROUP):
                first = PART * (GROUP * half + at)
                parts[b, half, at, pl.ds(0, PART), :] = tap_sum[b, pl.ds(first, PART), pl.ds(0, 128)]
                for side in range(2):
                    rest = tap_sum[b, pl.ds(first + 3 * side, 3), pl.ds(128, CH)]
                    parts[b, half, at, pl.ds(PART, 3), pl.ds(CH * side, CH)] = rest
        return across(parts.at[b, other_core], core_in.at[b], core_sems, b)

    def to_plane(b):
        parts[b, core] = parts[b, core] + core_in[b]
        return [
            send(parts.at[b, core, rank], scattered.at[b, step], plane_sems.at[b], step, device)
            for step, (device, rank) in enumerate(plane)
        ]

    def to_depth(b):
        total = parts[b, core, in_plane]
        for step in range(GROUP - 1):
            total = total + scattered[b, step]
        spread[b, depth] = total
        return [
            send(spread.at[b, depth], spread.at[b, depth], line_sems.at[b], step, device)
            for step, (device, _) in enumerate(line)
        ]

    def to_plane_again(b):
        total = spread[b, 0]
        for rank in range(1, DEPTH):
            total = total + spread[b, rank]
        gathered[b, core, in_plane] = total
        mine = gathered.at[b, core, in_plane]
        return [send(mine, mine, back_sems.at[b], step, device) for step, (device, _) in enumerate(plane)]

    def to_core_again(b):
        return across(gathered.at[b, core], gathered.at[b, core], core_sems, 2 + b)

    def grads_of(part):
        found = jnp.zeros((8, COLS), F32)
        for m in range(HERE):
            found += pull_apart(m, part)
        return found

    wait(shared[0])
    loss_tile = grads_of(0)
    over_rows(6, 4, lambda e: top(e, True))
    tap_grads(1, range(6, 10), True)
    backward(1, 7, None)
    wait(shared[1])
    loss_tile += grads_of(1)
    for e in (4, 5, 10, 11):
        top(e, True)
    tap_grads(1, (4, 5, 10, 11), False)
    core_1 = to_core(1)
    backward(1, 5, None)
    backward(1, 9, None)
    wait(core_1)
    plane_1 = to_plane(1)
    tap_grads(0, range(5, 11), True)
    wait(shared[2])
    grads_of(2)
    for e in (2, 3, 12, 13):
        top(e, False)
    for e in (3, 11):
        backward(1, e, None)
    tap_grads(0, (4, 11), False)
    core_0 = to_core(0)

    small[...] = jnp.zeros_like(small)
    sum_noise = tap_sum.at[0, pl.ds(0, CH), pl.ds(0, NOISE)]
    sum_noise[...] = jnp.zeros((CH, NOISE), F32)

    def last(e, m, entry_grad):
        sum_noise[...] += dot_rows(entry_grad, noise[e, m].astype(BF16))

    over(4, 2, lambda e: backward(0, e, last))
    wait(core_0)
    plane_0 = to_plane(0)
    over(8, 2, lambda e: backward(0, e, last))
    column = lax.broadcasted_iota(jnp.int32, (CH, NOISE), 1)
    late = sum_noise[...]
    rows = [as_row(jnp.sum(sums[at], axis=1, keepdims=True)) for at in range(5)]
    for k in range(NOISE):
        rows.append(as_row(jnp.sum(jnp.where(column == k, late, 0.0), axis=1, keepdims=True)))
    loss = jnp.sum(jnp.sum(loss_tile, axis=0, keepdims=True), axis=1, keepdims=True) * (0.5 / cells)
    rows.append(jnp.broadcast_to(loss, (1, CH)))
    for at, row in enumerate(rows):
        small[pl.ds(at // 2, 1), pl.ds(CH * (at % 2), CH)] = row
    small_0 = across(small, small_core, core_sems, 4)
    wait(plane_1)
    depth_1 = to_depth(1)
    wait(small_0)
    small_in[in_plane] = small[...] + small_core[...]
    mine = small_in.at[in_plane]
    small_1 = [send(mine, mine, small_sems, step, device) for step, (device, _) in enumerate(plane)]
    wait(plane_0)
    depth_0 = to_depth(0)
    wait(depth_1)
    back_1 = to_plane_again(1)
    wait(small_1)
    total = small_in[0]
    for rank in range(1, GROUP):
        total = total + small_in[rank]
    small_line[depth] = total
    mine = small_line.at[depth]
    small_2 = [send(mine, mine, small_line_sems, step, device) for step, (device, _) in enumerate(line)]
    wait(depth_0)
    back_0 = to_plane_again(0)
    wait(back_1)
    last_1 = to_core_again(1)
    wait(small_2)
    total = small_line[0]
    for rank in range(1, DEPTH):
        total = total + small_line[rank]
    small_out[...] = total
    wait(back_0)
    last_0 = to_core_again(0)
    wait(last_1 + last_0)


def unpack_kernel(
    predictions, gathered, small, loss, pred_out, grad_conv, grad_gain, grad_head, grad_head_gain, grad_noise, whole
):
    pred_out[...] = predictions[...]
    for b in range(2):
        for half in range(2):
            for at in range(GROUP):
                first = PART * (GROUP * half + at)
                whole[pl.ds(first, PART), pl.ds(0, 128)] = gathered[b, half, at, pl.ds(0, PART), :]
                for side in range(2):
                    rest = gathered[b, half, at, pl.ds(PART, 3), pl.ds(CH * side, CH)]
                    whole[pl.ds(first + 3 * side, 3), pl.ds(128, CH)] = rest
        for dr in range(3):
            for dc in range(3):
                grad_conv[b, 3 * dr + dc] = whole[pl.ds(CH * dc, CH), pl.ds(CH * dr, CH)]
    for out, first, count in ((grad_gain, 0, 2), (grad_head_gain, 2, 1), (grad_head, 3, 2), (grad_noise, 5, NOISE)):
        for at in range(count):
            out[pl.ds(at, 1), :] = small[pl.ds((first + at) // 2, 1), pl.ds(CH * ((first + at) % 2), CH)]
    loss[...] = small[pl.ds(6, 1), pl.ds(CH, 1)]


def on_device(
    block_input,
    member_seeds,
    targets,
    land_mask,
    noise_weight,
    conv_weight,
    block_gain,
    head_weight,
    head_gain,
):
    vmem = pl.BlockSpec(memory_space=pltpu.VMEM)
    far = pl.BlockSpec(memory_space=pltpu.HBM)

    def field(*shape):
        return pltpu.VMEM((EXT, HERE) + shape, F32)

    def half(*shape):
        return pltpu.VMEM((EXT, HERE) + shape, BF16)

    def sems(*shape):
        return pltpu.SemaphoreType.DMA(shape)

    scratch = dict(
        block_input=pltpu.VMEM(block_input.shape, BF16),
        seeds=pltpu.SMEM(member_seeds.shape, jnp.int32),
        targets=pltpu.VMEM(targets.shape, F32),
        land_mask=pltpu.VMEM(land_mask.shape, jnp.int32),
        noise_weight=pltpu.VMEM((NOISE, CH), BF16),
        conv_weight=pltpu.VMEM(conv_weight.shape, BF16),
        block_gain=pltpu.VMEM(block_gain.shape, F32),
        head_weight=pltpu.VMEM(head_weight.shape, BF16),
        head_gain=pltpu.VMEM((1, CH), F32),
        load_sems=sems(9),
        turned=pltpu.VMEM((HERE, 2, CH * ROWS, 128), F32),
        raw=half(CH, COLS),
        noise=field(NOISE, COLS),
        stream0=field(CH, COLS),
        stream1=field(CH, COLS),
        stream2=field(CH, COLS),
        inverse0=field(8, COLS),
        inverse1=field(8, COLS),
        inverse2=field(8, COLS),
        slope0=field(CH, COLS),
        slope1=field(CH, COLS),
        inputs0=half(CH, COLS),
        inputs1=half(CH, COLS),
        grads0=half(CH, COLS),
        grads1=half(CH, COLS),
        stream_grad=field(CH, COLS),
        head_in=half(CH, COLS),
        forward_taps=pltpu.VMEM((2, 6 * CH, 4 * CH), BF16),
        backward_taps=pltpu.VMEM((2, 6 * CH, 4 * CH), BF16),
        noise_taps=pltpu.VMEM((CH, NOISE), BF16),
        gains=pltpu.VMEM((5, CH, COLS), F32),
        edge_out=pltpu.VMEM((2, 8, COLS), F32),
        edge_in=pltpu.VMEM((2, 8, COLS), F32),
        target_tiles=pltpu.VMEM((3, 8, COLS), F32),
        weight_tiles=pltpu.VMEM((3, 8, COLS), F32),
        own_pred=pltpu.VMEM((3, HERE, 8, COLS), F32),
        all_pred=pltpu.VMEM((MEMS, 3, HERE, 8, COLS), F32),
        pred_grad=pltpu.VMEM((3, HERE, 8, COLS), F32),
        sums=pltpu.VMEM((5, CH, COLS), F32),
        tap_sum=pltpu.VMEM((2, 3 * CH + 8, 256), F32),
        parts=pltpu.VMEM((3, 2, GROUP, DENSE, 128), F32),
        core_in=pltpu.VMEM((2, GROUP, DENSE, 128), F32),
        scattered=pltpu.VMEM((2, GROUP - 1, DENSE, 128), F32),
        spread=pltpu.VMEM((2, DEPTH, DENSE, 128), F32),
        small=pltpu.VMEM((8, 128), F32),
        small_core=pltpu.VMEM((8, 128), F32),
        small_in=pltpu.VMEM((GROUP, 8, 128), F32),
        small_line=pltpu.VMEM((DEPTH, 8, 128), F32),
        halo_sems=sems(2, 6),
        mem_sems=sems(3, 2, MEMS - 1),
        core_sems=sems(2, 5),
        plane_sems=sems(2, 2, GROUP - 1),
        line_sems=sems(2, 2, DEPTH - 1),
        back_sems=sems(2, 2, GROUP - 1),
        small_sems=sems(2, GROUP - 1),
        small_line_sems=sems(2, DEPTH - 1),
    )
    predictions, gathered, small = pl.pallas_call(
        step_kernel,
        out_shape=(
            jax.ShapeDtypeStruct((HERE, 2, ROWS, COLS), F32),
            jax.ShapeDtypeStruct((2, 2, GROUP, DENSE, 128), F32),
            jax.ShapeDtypeStruct((8, 128), F32),
        ),
        in_specs=[far] * 9,
        out_specs=(vmem, vmem, vmem),
        scratch_shapes=list(scratch.values()),
        compiler_params=pltpu.CompilerParams(
            collective_id=0, has_side_effects=True, vmem_limit_bytes=VMEM_BYTES
        ),
        name="train_step",
    )(
        block_input,
        member_seeds,
        targets,
        land_mask,
        noise_weight.T,
        conv_weight,
        block_gain,
        head_weight,
        head_gain.reshape(1, CH),
    )
    loss, predictions, grad_conv, grad_block_gain, grad_head_weight, grad_head_gain, grad_noise = pl.pallas_call(
        unpack_kernel,
        out_shape=(
            jax.ShapeDtypeStruct((1, 1), F32),
            jax.ShapeDtypeStruct((HERE, 2, ROWS, COLS), F32),
            jax.ShapeDtypeStruct((2, 9, CH, CH), F32),
            jax.ShapeDtypeStruct((2, CH), F32),
            jax.ShapeDtypeStruct((2, CH), F32),
            jax.ShapeDtypeStruct((1, CH), F32),
            jax.ShapeDtypeStruct((NOISE, CH), F32),
        ),
        in_specs=[vmem] * 3,
        out_specs=(vmem,) * 7,
        scratch_shapes=[pltpu.VMEM((3 * CH + 8, 256), F32)],
        compiler_params=pltpu.CompilerParams(vmem_limit_bytes=VMEM_BYTES),
        name="unpack",
    )(predictions, gathered, small)
    return (
        loss.reshape(()),
        predictions,
        grad_conv,
        grad_block_gain,
        grad_head_weight,
        grad_head_gain.reshape(CH),
        grad_noise.T,
    )


def solution(mesh):
    return jax.shard_map(
        on_device,
        mesh=mesh,
        in_specs=(
            P("mem", None, "tile", None),
            P("mem"),
            P(None, "tile", None),
            P("tile", None),
            P(),
            P(),
            P(),
            P(),
            P(),
        ),
        out_specs=(P(), P("mem", None, "tile", None), P(), P(), P(), P(), P()),
        check_vma=False,
    )
```
